512 devices in a mesh: xy: 128 (over y, z, core), gz: 4 (over x).
Axes of the slice: x: 4, y: 8, z: 8, core: 2. Of those that a mesh axis runs over, the one named last changes fastest.
Arguments:
- material: int32 [16, 2048, 256], P('gz', 'xy'), may hold values from 0 to 7
- diffusivity: float32 [8], replicated, may hold values from 0.2 to 5
- variation: float32 [16, 2048, 256], P('gz', 'xy'), may hold values from 0.5 to 2
Outputs:
- stencil: float32 [27, 8, 1024, 128], P(None, 'gz', 'xy')
The draws below stay inside these ranges and needn't reach their ends.
Inputs may be any that keep to these rules, and one draw needn't show every extreme that they name: Each fine cell's material number is an integer from 0 to 7.
All inputs are finite; a program needn't handle non-finite values.
Results may differ from the reference program's by a relative error of at most 0.0003.
Values sent between devices are 32-bit elements; how exact they have to be, the bound alone decides.
A program may use at most 64 MiB of HBM per device.

```python
import math
import jax
import jax.numpy as jnp
from jax import lax

NY = 256
NMAT = 8
NZ = 16
NX = 2048


def touch_ends(entries, rng, smallest, largest):
    extent = entries.shape
    place = [jax.random.randint(jax.random.fold_in(rng, axis), (), 0, extent[axis]) for axis in range(len(extent))]
    entries = entries.at[tuple(place)].set(smallest)
    longest = extent.index(max(extent))
    place[longest] = (place[longest] + 1) % extent[longest]
    return entries.at[tuple(place)].set(largest)


def shard_levels(stream_key, shape, shards, smallest, high):
    level = 1.0
    for position, blocks in shards:
        steps = jax.random.uniform(jax.random.fold_in(jax.random.fold_in(stream_key, 6), position), (blocks,), jnp.float32, smallest / len(shards), high / len(shards))
        level = level * jnp.repeat(jnp.exp(steps), shape[position] // blocks).reshape((-1,) + (1,) * (len(shape) - 1 - position))
    return level


def setup_inputs(seed: int = 0) -> dict:
    key_of = jax.random.split(jax.random.key(seed), 4)
    material = touch_ends(jax.random.randint(key_of[0], (NZ, NX, NY), 0, NMAT), jax.random.fold_in(key_of[0], 1), 0, NMAT - 1).astype(jnp.int32)
    diffusivity = jnp.clip(jnp.exp(jax.random.uniform(key_of[1], (NMAT,), jnp.float32, math.log(0.2), math.log(5.0))), 0.2, 5.0)
    variation = jnp.clip(jnp.exp(math.log(2.0) - 1.3862944 * jax.random.uniform(key_of[2], (NZ, NX, NY), jnp.float32) ** shard_levels(key_of[2], (NZ, NX, NY), ((0, 4), (1, 128)), -0.2, 0.2)), 0.5, 2.0)
    return {"material": material, "diffusivity": diffusivity, "variation": variation}


def face_value(low_side, high_side, in_low, in_high):
    both_in = in_low & in_high
    face_sum = jnp.where(both_in, low_side + high_side, 1.0)
    harmonic = 2.0 * low_side * high_side / face_sum
    return jnp.where(both_in, harmonic, jnp.where(in_low, 2.0 * low_side, jnp.where(in_high, 2.0 * high_side, 0.0)))


def split_weights(low_face, high_face):
    face_sum = low_face + high_face
    safe_sum = jnp.where(face_sum > 0.0, face_sum, 1.0)
    return low_face / safe_sum, high_face / safe_sum


def refine(coarse, low_weight, high_weight, along):
    half_count = low_weight.shape[along]
    even_part = lax.slice_in_dim(coarse, 0, half_count, axis=along)
    next_part = lax.slice_in_dim(coarse, 1, half_count + 1, axis=along)
    odd_part = low_weight * even_part + high_weight * next_part
    paired = jnp.stack([even_part, odd_part], axis=along + 1)
    new_shape = list(even_part.shape)
    new_shape[along] = 2 * half_count
    return paired.reshape(new_shape)


def restrict(fine, low_weight, high_weight, along):
    half_count = low_weight.shape[along]
    new_shape = list(fine.shape)
    new_shape[along:along + 1] = [half_count, 2]
    paired = fine.reshape(new_shape)
    even_part = lax.index_in_dim(paired, 0, axis=along + 1, keepdims=False)
    odd_part = lax.index_in_dim(paired, 1, axis=along + 1, keepdims=False)
    pad_after = [(0, 0)] * fine.ndim
    pad_after[along] = (0, 1)
    pad_before = [(0, 0)] * fine.ndim
    pad_before[along] = (1, 0)
    return jnp.pad(even_part + low_weight * odd_part, pad_after) + jnp.pad(high_weight * odd_part, pad_before)


def prepare(kappa_pad, start_z, start_x, full_z, full_x):
    depth, width, span = kappa_pad.shape
    rows_z = start_z - 1 + jnp.arange(depth, dtype=jnp.int32)
    rows_x = start_x - 1 + jnp.arange(width, dtype=jnp.int32)
    rows_y = jnp.arange(span, dtype=jnp.int32) - 1
    inside = (((rows_z >= 0) & (rows_z < full_z))[:, None, None]
              & ((rows_x >= 0) & (rows_x < full_x))[None, :, None]
              & ((rows_y >= 0) & (rows_y < span - 2))[None, None, :])
    safe_kappa = jnp.where(inside, kappa_pad, 1.0)
    z_faces = face_value(safe_kappa[:-1], safe_kappa[1:], inside[:-1], inside[1:])
    x_faces = face_value(safe_kappa[:, :-1], safe_kappa[:, 1:], inside[:, :-1], inside[:, 1:])
    y_faces = face_value(safe_kappa[:, :, :-1], safe_kappa[:, :, 1:], inside[:, :, :-1], inside[:, :, 1:])
    weights_z = split_weights(z_faces[1::2, 1::2, 1::2], z_faces[2::2, 1::2, 1::2])
    weights_y = split_weights(y_faces[1:-1, 1::2, 1::2], y_faces[1:-1, 1::2, 2::2])
    weights_x = split_weights(x_faces[1:-1, 1::2, 1:-1], x_faces[1:-1, 2::2, 1:-1])
    face_z = z_faces[:, 1:-1, 1:-1]
    face_x = x_faces[1:-1, :, 1:-1]
    face_y = y_faces[1:-1, 1:-1, :]
    diagonal = face_z[:-1] + face_z[1:] + face_x[:, :-1] + face_x[:, 1:] + face_y[:, :, :-1] + face_y[:, :, 1:]
    window_inside = inside[1:-1, 1:-1, 1:-1].astype(jnp.float32)
    return weights_z, weights_y, weights_x, (face_z, face_x, face_y, diagonal), window_inside


def refine_probe(colour, setup, start_z, start_x, coarse_z, coarse_x):
    weights_z, weights_y, weights_x, stencil_faces, window_inside = setup
    depth, width, span = window_inside.shape
    level_z = start_z // 2 + jnp.arange(depth // 2 + 1, dtype=jnp.int32)
    level_x = start_x // 2 + jnp.arange(width // 2 + 1, dtype=jnp.int32)
    level_y = jnp.arange(span // 2 + 1, dtype=jnp.int32)
    pick_z = ((level_z % 3 == colour // 9) & (level_z >= 0) & (level_z < coarse_z)).astype(jnp.float32)
    pick_x = ((level_x % 3 == (colour // 3) % 3) & (level_x >= 0) & (level_x < coarse_x)).astype(jnp.float32)
    pick_y = ((level_y % 3 == colour % 3) & (level_y < span // 2)).astype(jnp.float32)
    probe = pick_z[:, None, None] * pick_x[None, :, None] * pick_y[None, None, :]
    field = refine(probe, weights_z[0], weights_z[1], 0)
    field = refine(field, weights_y[0], weights_y[1], 2)
    field = refine(field, weights_x[0], weights_x[1], 1)
    return field * window_inside


def coarse_image(padded, setup):
    weights_z, weights_y, weights_x, stencil_faces, window_inside = setup
    face_z, face_x, face_y, diagonal = stencil_faces
    center = padded[1:-1, 1:-1, 1:-1]
    image = diagonal * center
    image = image - face_z[:-1] * padded[:-2, 1:-1, 1:-1] - face_z[1:] * padded[2:, 1:-1, 1:-1]
    image = image - face_x[:, :-1] * padded[1:-1, :-2, 1:-1] - face_x[:, 1:] * padded[1:-1, 2:, 1:-1]
    image = image - face_y[:, :, :-1] * padded[1:-1, 1:-1, :-2] - face_y[:, :, 1:] * padded[1:-1, 1:-1, 2:]
    image = image * window_inside
    coarse = restrict(image, weights_x[0], weights_x[1], 1)
    coarse = restrict(coarse, weights_y[0], weights_y[1], 2)
    coarse = restrict(coarse, weights_z[0], weights_z[1], 0)
    return coarse[:, :, :window_inside.shape[2] // 2]


def assemble(stacked, level_z, level_x, level_y):
    parts = stacked.reshape((3, 3, 3) + stacked.shape[1:])
    offsets = jnp.arange(3, dtype=jnp.int32) - 1
    tones = jnp.arange(3, dtype=jnp.int32)
    match_z = (((level_z[None, None, :] + offsets[:, None, None]) % 3) == tones[None, :, None]).astype(jnp.float32)
    match_x = (((level_x[None, None, :] + offsets[:, None, None]) % 3) == tones[None, :, None]).astype(jnp.float32)
    match_y = (((level_y[None, None, :] + offsets[:, None, None]) % 3) == tones[None, :, None]).astype(jnp.float32)
    first = match_z[:, 0][:, None, None, :, None, None] * parts[0][None]
    for tone in range(1, 3):
        first = first + match_z[:, tone][:, None, None, :, None, None] * parts[tone][None]
    second = match_x[:, 0][None, :, None, None, :, None] * first[:, 0][:, None]
    for tone in range(1, 3):
        second = second + match_x[:, tone][None, :, None, None, :, None] * first[:, tone][:, None]
    third = match_y[:, 0][None, None, :, None, None, :] * second[:, :, 0][:, :, None]
    for tone in range(1, 3):
        third = third + match_y[:, tone][None, None, :, None, None, :] * second[:, :, tone][:, :, None]
    return third.reshape((27,) + stacked.shape[1:])


def reference(material, diffusivity, variation):
    base = jnp.zeros(material.shape, jnp.float32)
    for which in range(NMAT):
        base = base + jnp.where(material == which, diffusivity[which], jnp.float32(0.0))
    kappa = base * variation
    kappa_pad = jnp.pad(kappa, 1)
    setup = prepare(kappa_pad, 0, 0, NZ, NX)

    def colour_image(colour):
        fine_probe = refine_probe(colour, setup, 0, 0, NZ // 2, NX // 2)
        images = coarse_image(jnp.pad(fine_probe, 1), setup)
        return images[:NZ // 2, :NX // 2]

    stacked = lax.map(colour_image, jnp.arange(27, dtype=jnp.int32))
    return assemble(stacked, jnp.arange(NZ // 2, dtype=jnp.int32), jnp.arange(NX // 2, dtype=jnp.int32), jnp.arange(NY // 2, dtype=jnp.int32))
```

```python
import functools

import jax
import jax.numpy as jnp
from jax import lax
from jax.experimental import pallas as pl
from jax.experimental.pallas import tpu as pltpu
from jax.sharding import PartitionSpec as P

MESH = pl.DeviceIdType.MESH
OUTSIDE = -1e-18
STEPS = [(dz, dx) for dz in (-1, 0, 1) for dx in (-1, 0, 1) if (dz, dx) != (0, 0)]


class Rows:
    def __init__(self, own, edge):
        self.own, self.edge = own, edge

    def __add__(self, other):
        return Rows(self.own + other.own, self.edge + other.edge)

    def __mul__(self, other):
        return Rows(self.own * other.own, self.edge * other.edge)

    def map(self, function):
        return Rows(function(self.own), function(self.edge))


def row_index():
    return lax.broadcasted_iota(jnp.int32, (8, 128), 0)


def lane_index():
    return lax.broadcasted_iota(jnp.int32, (8, 128), 1)


def next_row(value):
    last = row_index() == 7
    own = pltpu.roll(value.own, 7, 0)
    edge = pltpu.roll(value.edge, 7, 0)
    return Rows(jnp.where(last, edge, own), jnp.where(last, own, edge))


def previous_row(value):
    first = row_index() == 0
    return jnp.where(first, pltpu.roll(value.edge, 1, 0), pltpu.roll(value.own, 1, 0))


def next_lane(value):
    return pltpu.roll(value, 127, 1)


def previous_lane(value):
    return pltpu.roll(value, 1, 1)


def next_lane_bounded(value):
    return jnp.where(lane_index() == 127, OUTSIDE, next_lane(value))


def previous_lane_bounded(value):
    return jnp.where(lane_index() == 0, OUTSIDE, previous_lane(value))


def without_last(value):
    return jnp.where(lane_index() == 127, 0.0, value)


def inverse(value):
    return 1.0 / value


class Plane:
    pass


def weights_of(load):
    plane = Plane()
    plane.rho = [[load(xp, yp) for yp in (0, 1)] for xp in (0, 1)]
    plane.low, plane.high, plane.link = [], [], []
    for yp in (0, 1):
        even, odd = plane.rho[0][yp], plane.rho[1][yp]
        before = even + odd
        after = odd + next_row(even)
        link = (before + after).map(inverse)
        plane.low.append(after * link)
        plane.high.append(before * link)
        plane.link.append(link)
    even, odd = plane.rho[0]
    plane.before = even + odd
    plane.after = odd + even.map(next_lane_bounded)
    scale = (plane.before + plane.after).map(inverse)
    plane.y_low = plane.after * scale
    plane.y_high = (plane.before * scale).map(without_last)
    plane.y_low_next = next_row(plane.y_low)
    plane.y_high_next = next_row(plane.y_high)
    return plane


def z_link(lower, upper):
    steps = []
    faces = []
    for yp in (0, 1):
        even = inverse(lower.rho[0][yp].own + upper.rho[0][yp].own)
        odd = (lower.rho[1][yp] + upper.rho[1][yp]).map(inverse)
        low, high = lower.low[yp] * odd, lower.high[yp] * odd
        same = even + (low * upper.low[yp]).own + previous_row(high * upper.high[yp])
        steps.append((same, low * upper.high[yp], high * upper.low[yp]))
        faces.append((even, odd))
    (even_same, even_up, even_down), (odd_same, odd_up, odd_down) = steps
    z = Plane()
    z.faces = faces
    first, second = lower.y_low.own * odd_same, lower.y_high.own * odd_same
    z.same = (
        even_same + first * upper.y_low.own + previous_lane(second * upper.y_high.own),
        first * upper.y_high.own,
        second * upper.y_low.own,
    )
    first, second = lower.y_low * odd_up, lower.y_high * odd_up
    z.up = (
        even_up + first * upper.y_low_next + (second * upper.y_high_next).map(previous_lane),
        first * upper.y_high_next,
        second * upper.y_low_next,
    )
    first, second = lower.y_low_next * odd_down, lower.y_high_next * odd_down
    z.down = (
        even_down + first * upper.y_low + (second * upper.y_high).map(previous_lane),
        first * upper.y_high,
        second * upper.y_low,
    )
    return z


def within(plane, faces_below, faces_above):
    even_before = inverse(plane.before.own)
    even_after = inverse(plane.after.own)
    (odd_e, odd_o) = plane.rho[1]
    odd_before = (odd_e + odd_o).map(inverse)
    odd_after = (odd_o + odd_e.map(next_lane_bounded)).map(inverse)

    def lower_face(face, rho):
        return jnp.where(lane_index() == 0, inverse(rho), previous_lane(face))

    even_lower = lower_face(even_after, plane.rho[0][0].own + OUTSIDE)
    odd_lower = Rows(
        lower_face(odd_after.own, odd_e.own + OUTSIDE),
        lower_face(odd_after.edge, odd_e.edge + OUTSIDE),
    )
    even_sum = [
        even_before + even_lower + faces_below[0][0] + faces_above[0][0],
        even_before + even_after + faces_below[1][0] + faces_above[1][0],
    ]
    odd_sum = [
        odd_before + odd_lower + faces_below[0][1] + faces_above[0][1],
        odd_before + odd_after + faces_below[1][1] + faces_above[1][1],
    ]
    centre, along = [], []
    for yp in (0, 1):
        low, high, link = plane.low[yp], plane.high[yp], plane.link[yp]
        low_sum, high_sum = low * odd_sum[yp], high * odd_sum[yp]
        centre.append(
            even_sum[yp]
            + (link + low_sum * low).own
            + previous_row(link + high_sum * high)
        )
        along.append(
            Rows(
                link.own - low_sum.own * high.own,
                link.edge - low_sum.edge * high.edge,
            )
        )
    even_after = without_last(even_after)
    odd_after = odd_after.map(without_last)
    low_e, low_o = plane.low
    high_e, high_o = plane.high
    low_n, high_n = low_e.map(next_lane), high_e.map(next_lane)
    first, second = low_o * odd_before, high_o * odd_before
    before = (
        even_before + (first * low_e).own + previous_row(second * high_e),
        second * low_e,
        first * high_e,
    )
    first, second = low_o * odd_after, high_o * odd_after
    after = (
        even_after + (first * low_n).own + previous_row(second * high_n),
        first * high_n,
        second * low_n,
    )
    low, high = plane.y_low, plane.y_high
    low_next, high_next = plane.y_low_next, plane.y_high_next
    c = Plane()
    cross = low.own * centre[1]
    c.side = high.own * before[0] + low.own * after[0] - cross * high.own
    c.centre = (
        centre[0]
        + low.own * (cross - before[0] - before[0])
        + previous_lane(high.own * (high.own * centre[1] - after[0] - after[0]))
    )
    one = low * along[1] + before[1]
    two = high * along[1] + after[2]
    c.up = (
        along[0]
        + low_next * one
        + low * before[2]
        + (high_next * two + high * after[1]).map(previous_lane),
        high_next * one + low * after[1],
        low_next * two + high * before[2],
    )
    return c


def z_weights(below, middle, above):
    before = below.rho[0][0] + middle.rho[0][0]
    after = middle.rho[0][0] + above.rho[0][0]
    scale = (before + after).map(inverse)

    def versions(value):
        lane = value.map(next_lane)
        row = next_row(value)
        return (value, lane, row, row.map(next_lane))

    return versions(after * scale), versions(before * scale)


def between(weights, inner, low_link, high_link):
    (lo, lo_j, lo_i, lo_ij), (hi, hi_j, hi_i, hi_ij) = weights

    def term(first, second, low, high, own):
        return second * (low + first * own) + first * high

    same = (
        hi.own * (low_link.same[0] - lo.own * inner.centre) + lo.own * high_link.same[0],
        term(lo.own, hi_j.own, low_link.same[1], high_link.same[1], inner.side),
        term(lo_j.own, hi.own, low_link.same[2], high_link.same[2], inner.side),
    )
    up = (
        term(lo, hi_i, low_link.up[0], high_link.up[0], inner.up[0]),
        term(lo, hi_ij, low_link.up[1], high_link.up[1], inner.up[1]),
        term(lo_j, hi_i, low_link.up[2], high_link.up[2], inner.up[2]),
    )
    down = (
        term(lo_i, hi, low_link.down[0], high_link.down[0], inner.up[0]),
        term(lo_i, hi_j, low_link.down[1], high_link.down[1], inner.up[2]),
        term(lo_ij, hi, low_link.down[2], high_link.down[2], inner.up[1]),
    )
    return same, up, down


def level(own, below, above):
    centre, side = own.centre, own.side
    up = list(own.up)
    (_, hi), inner, link = below
    hi, hi_j, hi_i, hi_ij = hi
    centre = centre + hi.own * (hi.own * inner.centre - link.same[0] - link.same[0])
    side = side + hi.own * (hi_j.own * inner.side + link.same[1]) + hi_j.own * link.same[2]
    up[0] = up[0] + hi * (hi_i * inner.up[0] + link.up[0]) + hi_i * link.down[0]
    up[1] = up[1] + hi * (hi_ij * inner.up[1] + link.up[1]) + hi_ij * link.down[2]
    up[2] = up[2] + hi_j * (hi_i * inner.up[2] + link.up[2]) + hi_i * link.down[1]
    (lo, _), inner, link = above
    lo, lo_j, lo_i, lo_ij = lo
    centre = centre + lo.own * (lo.own * inner.centre - link.same[0] - link.same[0])
    side = side + lo_j.own * (lo.own * inner.side + link.same[1]) + lo.own * link.same[2]
    up[0] = up[0] + lo_i * (lo * inner.up[0] + link.up[0]) + lo * link.down[0]
    up[1] = up[1] + lo_ij * (lo * inner.up[1] + link.up[1]) + lo * link.down[2]
    up[2] = up[2] + lo_i * (lo_j * inner.up[2] + link.up[2]) + lo_j * link.down[1]
    return centre, side, up


def stencil_of(load, store):
    planes = [weights_of(functools.partial(load, p)) for p in range(7)]
    links = [z_link(planes[p], planes[p + 1]) for p in range(6)]
    inner = [None] * 7
    for p in range(1, 6):
        inner[p] = within(planes[p], links[p - 1].faces, links[p].faces)
    weights = [None] * 7
    for p in (1, 3, 5):
        weights[p] = z_weights(planes[p - 1], planes[p], planes[p + 1])
    for p in (1, 3, 5):
        same, up, down = between(weights[p], inner[p], links[p - 1], links[p])
        plane = (p - 1) // 2
        if plane < 2:
            low = functools.partial(store, -1)
            low(0, 0, plane, same[0])
            low(0, 1, plane, same[2])
            low(0, -1, plane, previous_lane(same[1]))
            low(1, 0, plane, down[0].own)
            low(1, 1, plane, down[2].own)
            low(1, -1, plane, previous_lane(down[1].own))
            low(-1, 0, plane, previous_row(up[0]))
            low(-1, 1, plane, previous_row(up[2]))
            low(-1, -1, plane, previous_lane(previous_row(up[1])))
        if plane > 0:
            high = functools.partial(store, 1)
            high(0, 0, plane - 1, same[0])
            high(0, 1, plane - 1, same[1])
            high(0, -1, plane - 1, previous_lane(same[2]))
            high(1, 0, plane - 1, up[0].own)
            high(1, 1, plane - 1, up[1].own)
            high(1, -1, plane - 1, previous_lane(up[2].own))
            high(-1, 0, plane - 1, previous_row(down[0]))
            high(-1, 1, plane - 1, previous_row(down[1]))
            high(-1, -1, plane - 1, previous_lane(previous_row(down[2])))
    for plane in (0, 1):
        p = 2 * plane + 2
        centre, side, up = level(
            inner[p],
            (weights[p - 1], inner[p - 1], links[p - 1]),
            (weights[p + 1], inner[p + 1], links[p]),
        )
        here = functools.partial(store, 0)
        here(0, 0, plane, -centre)
        here(0, 1, plane, side)
        here(0, -1, plane, previous_lane(side))
        here(1, 0, plane, up[0].own)
        here(-1, 0, plane, previous_row(up[0]))
        here(1, 1, plane, up[1].own)
        here(-1, -1, plane, previous_lane(previous_row(up[1])))
        here(1, -1, plane, previous_lane(up[2].own))
        here(-1, 1, plane, previous_row(up[2]))


def split_lanes(value):
    lane = lax.broadcasted_iota(jnp.int32, (16, 128), 1)
    left, right = value[:, :128], value[:, 128:]
    first = (lane * 2) % 128 + lane // 64
    left = jnp.take_along_axis(left, first, axis=1)
    right = jnp.take_along_axis(right, (first + 1) % 2 + first // 2 * 2, axis=1)
    even = jnp.where(lane < 64, left, right)
    odd = pltpu.roll(jnp.where(lane < 64, right, left), 64, 1)
    return even, odd


def exchange_kernel(material, diffusivity, variation, out, split, send_sem, recv_sem):
    gz, xy = lax.axis_index("gz"), lax.axis_index("xy")
    count_z, count_x = lax.axis_size("gz"), lax.axis_size("xy")

    def device(dz, dx):
        return {
            "gz": lax.rem(gz + (dz + count_z), count_z),
            "xy": lax.rem(xy + (dx + count_x), count_x),
        }

    barrier = pltpu.get_barrier_semaphore()
    for dz, dx in STEPS:
        pl.semaphore_signal(barrier, inc=1, device_id=device(dz, dx), device_id_type=MESH)

    table = [diffusivity[which] for which in range(8)]
    for k in range(4):
        which = material[k]
        bits = [(which & bit) != 0 for bit in (1, 2, 4)]
        values = table
        for bit in bits:
            values = [
                jnp.where(bit, values[2 * n + 1], values[2 * n])
                for n in range(len(values) // 2)
            ]
        rho = -0.5 / (values[0] * variation[k])
        for yp, half in enumerate(split_lanes(rho)):
            split[k, yp] = half
            for xp in (0, 1):
                out[0, k + 2, xp, yp] = split[k, yp, pl.ds(xp, 8, stride=2), :]

    pl.semaphore_wait(barrier, len(STEPS))
    copies = []
    for n, (dz, dx) in enumerate(STEPS):
        source = {-1: pl.ds(2, 1), 0: pl.ds(2, 4), 1: pl.ds(4, 2)}[dz]
        target = {-1: pl.ds(6, 1), 0: pl.ds(2, 4), 1: pl.ds(0, 2)}[dz]
        if dx == 0:
            src, dst = out.at[0, source], out.at[0, target]
        elif dx == 1:
            rows = (slice(None), slice(None), pl.ds(7, 1))
            src, dst = out.at[(0, source) + rows], out.at[(1, target) + rows]
        else:
            rows = (0, slice(None), pl.ds(0, 1))
            src, dst = out.at[(0, source) + rows], out.at[(1, target) + rows]
        copy = pltpu.make_async_remote_copy(
            src_ref=src,
            dst_ref=dst,
            send_sem=send_sem.at[n],
            recv_sem=recv_sem.at[n],
            device_id=device(dz, dx),
            device_id_type=MESH,
        )
        copy.start()
        copies.append(copy)
    for copy in copies:
        copy.wait()

    @pl.when(gz == 0)
    def _():
        out[:, 0:2] = jnp.full((2, 2, 2, 2, 8, 128), OUTSIDE, jnp.float32)

    @pl.when(gz == count_z - 1)
    def _():
        out[:, 6] = jnp.full((2, 2, 2, 8, 128), OUTSIDE, jnp.float32)

    @pl.when(xy == 0)
    def _():
        out[1, :, :, :, 7, :] = jnp.full((7, 2, 2, 128), OUTSIDE, jnp.float32)

    @pl.when(xy == count_x - 1)
    def _():
        out[1, :, 0, :, 0, :] = jnp.full((7, 2, 128), OUTSIDE, jnp.float32)


def stencil_kernel(rho, out):
    gz, xy = lax.axis_index("gz"), lax.axis_index("xy")

    def load(p, xp, yp):
        return Rows(rho[0, p, xp, yp], rho[1, p, xp, yp])

    def store(dz, dx, dy, plane, value):
        out[9 * (dz + 1) + 3 * (dx + 1) + dy + 1, plane] = value

    stencil_of(load, store)
    nothing = jnp.zeros((1, 128), jnp.float32)

    def clear_row(dx, row):
        for dz in (-1, 0, 1):
            for dy in (-1, 0, 1):
                for plane in (0, 1):
                    entry = 9 * (dz + 1) + 3 * (dx + 1) + dy + 1
                    out[entry, plane, pl.ds(row, 1), :] = nothing

    @pl.when(xy == 0)
    def _():
        clear_row(-1, 0)

    @pl.when(xy == lax.axis_size("xy") - 1)
    def _():
        clear_row(1, 7)

    @pl.when(gz == 0)
    def _():
        out[0:9, 0] = jnp.zeros((9, 8, 128), jnp.float32)

    @pl.when(gz == lax.axis_size("gz") - 1)
    def _():
        out[18:27, 1] = jnp.zeros((9, 8, 128), jnp.float32)


def per_device(material, diffusivity, variation):
    vmem = pl.BlockSpec(memory_space=pltpu.VMEM)
    rho = pl.pallas_call(
        exchange_kernel,
        out_shape=jax.ShapeDtypeStruct((2, 7, 2, 2, 8, 128), jnp.float32),
        in_specs=[vmem, pl.BlockSpec(memory_space=pltpu.SMEM), vmem],
        out_specs=vmem,
        scratch_shapes=[
            pltpu.VMEM((4, 2, 16, 128), jnp.float32),
            pltpu.SemaphoreType.DMA((len(STEPS),)),
            pltpu.SemaphoreType.DMA((len(STEPS),)),
        ],
        compiler_params=pltpu.CompilerParams(collective_id=0, has_side_effects=True),
        name="exchange",
    )(material, diffusivity, variation)
    return pl.pallas_call(
        stencil_kernel,
        out_shape=jax.ShapeDtypeStruct((27, 2, 8, 128), jnp.float32),
        in_specs=[vmem],
        out_specs=vmem,
        name="stencil",
    )(rho)


def solution(mesh):
    placed = (P("gz", "xy", None), P(), P("gz", "xy", None))
    return jax.shard_map(
        per_device, mesh=mesh, in_specs=placed, out_specs=P(None, "gz", "xy", None), check_vma=False
    )
```

```python
import functools

import jax
import jax.numpy as jnp
from jax import lax
from jax.experimental import pallas as pl
from jax.experimental.pallas import tpu as pltpu
from jax.sharding import PartitionSpec as P

MESH = pl.DeviceIdType.MESH
OUTSIDE = -1e-18
ROW = 16


class Rows:
    def __init__(self, own, edge):
        self.own, self.edge = own, edge

    def __add__(self, other):
        return Rows(self.own + other.own, self.edge + other.edge)

    def __mul__(self, other):
        return Rows(self.own * other.own, self.edge * other.edge)

    def map(self, function):
        return Rows(function(self.own), function(self.edge))


def row_index():
    return lax.broadcasted_iota(jnp.int32, (8, 128), 0)


def lane_index():
    return lax.broadcasted_iota(jnp.int32, (8, 128), 1)


def next_row(value):
    last = row_index() == 7
    own = pltpu.roll(value.own, 7, 0)
    edge = pltpu.roll(value.edge, 7, 0)
    return Rows(jnp.where(last, edge, own), jnp.where(last, own, edge))


def previous_row(value):
    first = row_index() == 0
    return jnp.where(first, pltpu.roll(value.edge, 1, 0), pltpu.roll(value.own, 1, 0))


def next_lane(value):
    return pltpu.roll(value, 127, 1)


def previous_lane(value):
    return pltpu.roll(value, 1, 1)


def next_lane_bounded(value):
    return jnp.where(lane_index() == 127, OUTSIDE, next_lane(value))


def previous_lane_bounded(value):
    return jnp.where(lane_index() == 0, OUTSIDE, previous_lane(value))


def without_last(value):
    return jnp.where(lane_index() == 127, 0.0, value)


def inverse(value):
    return 1.0 / value


class Plane:
    pass


def weights_of(load):
    plane = Plane()
    plane.rho = [[load(xp, yp) for yp in (0, 1)] for xp in (0, 1)]
    plane.low, plane.high, plane.link = [], [], []
    for yp in (0, 1):
        even, odd = plane.rho[0][yp], plane.rho[1][yp]
        before = even + odd
        after = odd + next_row(even)
        link = (before + after).map(inverse)
        plane.low.append(after * link)
        plane.high.append(before * link)
        plane.link.append(link)
    even, odd = plane.rho[0]
    plane.before = even + odd
    plane.after = odd + even.map(next_lane_bounded)
    scale = (plane.before + plane.after).map(inverse)
    plane.y_low = plane.after * scale
    plane.y_high = (plane.before * scale).map(without_last)
    plane.y_low_next = next_row(plane.y_low)
    plane.y_high_next = next_row(plane.y_high)
    return plane


def z_link(lower, upper):
    steps = []
    faces = []
    for yp in (0, 1):
        even = inverse(lower.rho[0][yp].own + upper.rho[0][yp].own)
        odd = (lower.rho[1][yp] + upper.rho[1][yp]).map(inverse)
        low, high = lower.low[yp] * odd, lower.high[yp] * odd
        same = even + (low * upper.low[yp]).own + previous_row(high * upper.high[yp])
        steps.append((same, low * upper.high[yp], high * upper.low[yp]))
        faces.append((even, odd))
    (even_same, even_up, even_down), (odd_same, odd_up, odd_down) = steps
    z = Plane()
    z.faces = faces
    first, second = lower.y_low.own * odd_same, lower.y_high.own * odd_same
    z.same = (
        even_same + first * upper.y_low.own + previous_lane(second * upper.y_high.own),
        first * upper.y_high.own,
        second * upper.y_low.own,
    )
    first, second = lower.y_low * odd_up, lower.y_high * odd_up
    z.up = (
        even_up + first * upper.y_low_next + (second * upper.y_high_next).map(previous_lane),
        first * upper.y_high_next,
        second * upper.y_low_next,
    )
    first, second = lower.y_low_next * odd_down, lower.y_high_next * odd_down
    z.down = (
        even_down + first * upper.y_low + (second * upper.y_high).map(previous_lane),
        first * upper.y_high,
        second * upper.y_low,
    )
    return z


def within(plane, faces_below, faces_above):
    even_before = inverse(plane.before.own)
    even_after = inverse(plane.after.own)
    (odd_e, odd_o) = plane.rho[1]
    odd_before = (odd_e + odd_o).map(inverse)
    odd_after = (odd_o + odd_e.map(next_lane_bounded)).map(inverse)

    def lower_face(face, rho):
        return jnp.where(lane_index() == 0, inverse(rho), previous_lane(face))

    even_lower = lower_face(even_after, plane.rho[0][0].own + OUTSIDE)
    odd_lower = Rows(
        lower_face(odd_after.own, odd_e.own + OUTSIDE),
        lower_face(odd_after.edge, odd_e.edge + OUTSIDE),
    )
    even_sum = [
        even_before + even_lower + faces_below[0][0] + faces_above[0][0],
        even_before + even_after + faces_below[1][0] + faces_above[1][0],
    ]
    odd_sum = [
        odd_before + odd_lower + faces_below[0][1] + faces_above[0][1],
        odd_before + odd_after + faces_below[1][1] + faces_above[1][1],
    ]
    centre, along = [], []
    for yp in (0, 1):
        low, high, link = plane.low[yp], plane.high[yp], plane.link[yp]
        low_sum, high_sum = low * odd_sum[yp], high * odd_sum[yp]
        centre.append(
            even_sum[yp]
            + (link + low_sum * low).own
            + previous_row(link + high_sum * high)
        )
        along.append(
            Rows(
                link.own - low_sum.own * high.own,
                link.edge - low_sum.edge * high.edge,
            )
        )
    even_after = without_last(even_after)
    odd_after = odd_after.map(without_last)
    low_e, low_o = plane.low
    high_e, high_o = plane.high
    low_n, high_n = low_e.map(next_lane), high_e.map(next_lane)
    first, second = low_o * odd_before, high_o * odd_before
    before = (
        even_before + (first * low_e).own + previous_row(second * high_e),
        second * low_e,
        first * high_e,
    )
    first, second = low_o * odd_after, high_o * odd_after
    after = (
        even_after + (first * low_n).own + previous_row(second * high_n),
        first * high_n,
        second * low_n,
    )
    low, high = plane.y_low, plane.y_high
    low_next, high_next = plane.y_low_next, plane.y_high_next
    c = Plane()
    cross = low.own * centre[1]
    c.side = high.own * before[0] + low.own * after[0] - cross * high.own
    c.centre = (
        centre[0]
        + low.own * (cross - before[0] - before[0])
        + previous_lane(high.own * (high.own * centre[1] - after[0] - after[0]))
    )
    one = low * along[1] + before[1]
    two = high * along[1] + after[2]
    c.up = (
        along[0]
        + low_next * one
        + low * before[2]
        + (high_next * two + high * after[1]).map(previous_lane),
        high_next * one + low * after[1],
        low_next * two + high * before[2],
    )
    return c


def z_weights(below, middle, above):
    before = below.rho[0][0] + middle.rho[0][0]
    after = middle.rho[0][0] + above.rho[0][0]
    scale = (before + after).map(inverse)

    def versions(value):
        lane = value.map(next_lane)
        row = next_row(value)
        return (value, lane, row, row.map(next_lane))

    return versions(after * scale), versions(before * scale)


def between(weights, inner, low_link, high_link):
    (lo, lo_j, lo_i, lo_ij), (hi, hi_j, hi_i, hi_ij) = weights

    def term(first, second, low, high, own):
        return second * (low + first * own) + first * high

    same = (
        hi.own * (low_link.same[0] - lo.own * inner.centre) + lo.own * high_link.same[0],
        term(lo.own, hi_j.own, low_link.same[1], high_link.same[1], inner.side),
        term(lo_j.own, hi.own, low_link.same[2], high_link.same[2], inner.side),
    )
    up = (
        term(lo, hi_i, low_link.up[0], high_link.up[0], inner.up[0]),
        term(lo, hi_ij, low_link.up[1], high_link.up[1], inner.up[1]),
        term(lo_j, hi_i, low_link.up[2], high_link.up[2], inner.up[2]),
    )
    down = (
        term(lo_i, hi, low_link.down[0], high_link.down[0], inner.up[0]),
        term(lo_i, hi_j, low_link.down[1], high_link.down[1], inner.up[2]),
        term(lo_ij, hi, low_link.down[2], high_link.down[2], inner.up[1]),
    )
    return same, up, down


def level(own, below, above):
    centre, side = own.centre, own.side
    up = list(own.up)
    (_, hi), inner, link = below
    hi, hi_j, hi_i, hi_ij = hi
    centre = centre + hi.own * (hi.own * inner.centre - link.same[0] - link.same[0])
    side = side + hi.own * (hi_j.own * inner.side + link.same[1]) + hi_j.own * link.same[2]
    up[0] = up[0] + hi * (hi_i * inner.up[0] + link.up[0]) + hi_i * link.down[0]
    up[1] = up[1] + hi * (hi_ij * inner.up[1] + link.up[1]) + hi_ij * link.down[2]
    up[2] = up[2] + hi_j * (hi_i * inner.up[2] + link.up[2]) + hi_i * link.down[1]
    (lo, _), inner, link = above
    lo, lo_j, lo_i, lo_ij = lo
    centre = centre + lo.own * (lo.own * inner.centre - link.same[0] - link.same[0])
    side = side + lo_j.own * (lo.own * inner.side + link.same[1]) + lo.own * link.same[2]
    up[0] = up[0] + lo_i * (lo * inner.up[0] + link.up[0]) + lo * link.down[0]
    up[1] = up[1] + lo_ij * (lo * inner.up[1] + link.up[1]) + lo * link.down[2]
    up[2] = up[2] + lo_i * (lo_j * inner.up[2] + link.up[2]) + lo_j * link.down[1]
    return centre, side, up


def stencil_of(load, store):
    planes = [weights_of(functools.partial(load, p)) for p in range(7)]
    links = [z_link(planes[p], planes[p + 1]) for p in range(6)]
    inner = [None] * 7
    for p in range(1, 6):
        inner[p] = within(planes[p], links[p - 1].faces, links[p].faces)
    weights = [None] * 7
    for p in (1, 3, 5):
        weights[p] = z_weights(planes[p - 1], planes[p], planes[p + 1])
    for p in (1, 3, 5):
        same, up, down = between(weights[p], inner[p], links[p - 1], links[p])
        plane = (p - 1) // 2
        if plane < 2:
            low = functools.partial(store, -1)
            low(0, 0, plane, same[0])
            low(0, 1, plane, same[2])
            low(0, -1, plane, previous_lane(same[1]))
            low(1, 0, plane, down[0].own)
            low(1, 1, plane, down[2].own)
            low(1, -1, plane, previous_lane(down[1].own))
            low(-1, 0, plane, previous_row(up[0]))
            low(-1, 1, plane, previous_row(up[2]))
            low(-1, -1, plane, previous_lane(previous_row(up[1])))
        if plane > 0:
            high = functools.partial(store, 1)
            high(0, 0, plane - 1, same[0])
            high(0, 1, plane - 1, same[1])
            high(0, -1, plane - 1, previous_lane(same[2]))
            high(1, 0, plane - 1, up[0].own)
            high(1, 1, plane - 1, up[1].own)
            high(1, -1, plane - 1, previous_lane(up[2].own))
            high(-1, 0, plane - 1, previous_row(down[0]))
            high(-1, 1, plane - 1, previous_row(down[1]))
            high(-1, -1, plane - 1, previous_lane(previous_row(down[2])))
    for plane in (0, 1):
        p = 2 * plane + 2
        centre, side, up = level(
            inner[p],
            (weights[p - 1], inner[p - 1], links[p - 1]),
            (weights[p + 1], inner[p + 1], links[p]),
        )
        here = functools.partial(store, 0)
        here(0, 0, plane, -centre)
        here(0, 1, plane, side)
        here(0, -1, plane, previous_lane(side))
        here(1, 0, plane, up[0].own)
        here(-1, 0, plane, previous_row(up[0]))
        here(1, 1, plane, up[1].own)
        here(-1, -1, plane, previous_lane(previous_row(up[1])))
        here(1, -1, plane, previous_lane(up[2].own))
        here(-1, 1, plane, previous_row(up[2]))


def split_lanes(value):
    lane = lax.broadcasted_iota(jnp.int32, (value.shape[0], 128), 1)
    left, right = value[:, :128], value[:, 128:]
    first = (lane * 2) % 128 + lane // 64
    left = jnp.take_along_axis(left, first, axis=1)
    right = jnp.take_along_axis(right, (first + 1) % 2 + first // 2 * 2, axis=1)
    even = jnp.where(lane < 64, left, right)
    odd = pltpu.roll(jnp.where(lane < 64, right, left), 64, 1)
    return even, odd


SENT = {-1: (0, 1), 0: (0, 4), 1: (2, 2)}
LANDED = {-1: 6, 0: 2, 1: 0}
AHEAD = [(0, 1), (-1, 1), (1, 1)]
SIDE = [(-1, 0), (1, 0)]
BACK = [(0, -1), (-1, -1), (1, -1)]
MESSAGES = AHEAD + SIDE + BACK


def exchange_kernel(
    material, diffusivity, variation, out, blocks, facts, borders, edges, split, load_sem, send_sem, recv_sem
):
    gz, xy = lax.axis_index("gz"), lax.axis_index("xy")
    count_z, count_x = lax.axis_size("gz"), lax.axis_size("xy")
    inputs = (material, variation)
    own = (blocks, facts)

    def exists(dz, dx):
        inside = None
        for at, step, count in ((gz, dz, count_z), (xy, dx, count_x)):
            if step:
                good = at + step < count if step > 0 else at > 0
                inside = good if inside is None else jnp.logical_and(inside, good)
        return inside

    def device(dz, dx):
        return {"gz": gz + dz, "xy": xy + dx}

    def copies(dz, dx):
        n = MESSAGES.index((dz, dx))
        first, planes = SENT[dz]
        made = []
        for which in (0, 1):
            source = inputs[which].at[pl.ds(first, planes)]
            if dx == 0:
                target = borders[which].at[pl.ds(0 if dz > 0 else 2, planes)]
            else:
                row, rows, at = (14, 2, 6) if dx > 0 else (0, 1, 0)
                source = inputs[which].at[pl.ds(first, planes), pl.ds(row, rows)]
                target = edges[which].at[pl.ds(LANDED[dz], planes), pl.ds(at, rows)]
            made.append(
                pltpu.make_async_remote_copy(
                    src_ref=source,
                    dst_ref=target,
                    send_sem=send_sem.at[n, which],
                    recv_sem=recv_sem.at[n, which],
                    device_id=device(dz, dx),
                    device_id_type=MESH,
                )
            )
        return made

    def send(dz, dx, condition=None):
        good = exists(dz, dx)

        @pl.when(good if condition is None else jnp.logical_and(good, condition))
        def _():
            for copy in copies(dz, dx):
                copy.start()

    def receive(dz, dx):
        @pl.when(exists(-dz, -dx))
        def _():
            for copy in copies(dz, dx):
                copy.wait_recv()

    barrier = pltpu.get_barrier_semaphore()
    last = jnp.logical_and(lax.rem(xy, ROW) == ROW - 1, xy < count_x - 1)

    def greet(dz, dx, condition=None):
        good = exists(dz, dx)

        @pl.when(good if condition is None else jnp.logical_and(good, condition))
        def _():
            pl.semaphore_signal(barrier, inc=1, device_id=device(dz, dx), device_id_type=MESH)

    for dz, dx in BACK:
        greet(dz, dx)
    for dz, dx in SIDE:
        greet(dz, dx, jnp.logical_not(last))
    loads = [pltpu.make_async_copy(inputs[n], own[n], load_sem.at[n]) for n in (0, 1)]
    for copy in loads:
        copy.start()
    one = jnp.int32(1)
    z_sides = jnp.where(gz > 0, one, 0) + jnp.where(gz < count_z - 1, one, 0)
    expected = jnp.where(last, 0, z_sides) + jnp.where(xy < count_x - 1, z_sides + 1, 0)
    pl.semaphore_wait(barrier, expected)
    for dz, dx in AHEAD:
        send(dz, dx)
    for dz, dx in SIDE:
        send(dz, dx, jnp.logical_not(last))

    table = [diffusivity[which] for which in range(8)]

    def resistivity(which, factor):
        values = table
        for bit in (1, 2, 4):
            chosen = (which & bit) != 0
            values = [
                jnp.where(chosen, values[2 * n + 1], values[2 * n])
                for n in range(len(values) // 2)
            ]
        return -0.5 / (values[0] * factor)

    def place(plane, which, factor):
        for yp, half in enumerate(split_lanes(resistivity(which, factor))):
            split[plane, yp] = half
            for xp in (0, 1):
                out[0, plane, xp, yp] = split[plane, yp, pl.ds(xp, 8, stride=2), :]

    for copy in loads:
        copy.wait()
    for k in range(4):
        place(k + 2, blocks[k], facts[k])

    @pl.when(last)
    def _():
        for dz, dx in AHEAD:
            receive(dz, dx)
        for dz, dx in BACK:
            send(dz, dx)
        for dz, dx in SIDE:
            send(dz, dx)

    for dz, dx in SIDE:
        receive(dz, dx)
    for n, plane in enumerate((0, 1, 6)):
        place(plane, borders[0][n], borders[1][n])

    @pl.when(jnp.logical_not(last))
    def _():
        for dz, dx in AHEAD:
            receive(dz, dx)
        for dz, dx in BACK:
            send(dz, dx)

    for dz, dx in BACK:
        receive(dz, dx)
    bottom = row_index() == 7
    for plane in range(7):
        halves = split_lanes(resistivity(edges[0][plane], edges[1][plane]))
        for yp, half in enumerate(halves):
            out[1, plane, 0, yp] = jnp.where(bottom, pltpu.roll(half, 1, 0), half)
            out[1, plane, 1, yp] = half
    for dz, dx in MESSAGES:
        @pl.when(exists(dz, dx))
        def _():
            for copy in copies(dz, dx):
                copy.wait_send()

    @pl.when(gz == 0)
    def _():
        out[:, 0:2] = jnp.full((2, 2, 2, 2, 8, 128), OUTSIDE, jnp.float32)

    @pl.when(gz == count_z - 1)
    def _():
        out[:, 6] = jnp.full((2, 2, 2, 8, 128), OUTSIDE, jnp.float32)

    @pl.when(xy == 0)
    def _():
        out[1, :, :, :, 7, :] = jnp.full((7, 2, 2, 128), OUTSIDE, jnp.float32)

    @pl.when(xy == count_x - 1)
    def _():
        out[1, :, 0, :, 0, :] = jnp.full((7, 2, 128), OUTSIDE, jnp.float32)


def stencil_kernel(rho, out):
    gz, xy = lax.axis_index("gz"), lax.axis_index("xy")

    def load(p, xp, yp):
        return Rows(rho[0, p, xp, yp], rho[1, p, xp, yp])

    def store(dz, dx, dy, plane, value):
        out[9 * (dz + 1) + 3 * (dx + 1) + dy + 1, plane] = value

    stencil_of(load, store)
    nothing = jnp.zeros((1, 128), jnp.float32)

    def clear_row(dx, row):
        for dz in (-1, 0, 1):
            for dy in (-1, 0, 1):
                for plane in (0, 1):
                    entry = 9 * (dz + 1) + 3 * (dx + 1) + dy + 1
                    out[entry, plane, pl.ds(row, 1), :] = nothing

    @pl.when(xy == 0)
    def _():
        clear_row(-1, 0)

    @pl.when(xy == lax.axis_size("xy") - 1)
    def _():
        clear_row(1, 7)

    @pl.when(gz == 0)
    def _():
        out[0:9, 0] = jnp.zeros((9, 8, 128), jnp.float32)

    @pl.when(gz == lax.axis_size("gz") - 1)
    def _():
        out[18:27, 1] = jnp.zeros((9, 8, 128), jnp.float32)


def per_device(material, diffusivity, variation):
    vmem = pl.BlockSpec(memory_space=pltpu.VMEM)
    rho = pl.pallas_call(
        exchange_kernel,
        out_shape=jax.ShapeDtypeStruct((2, 7, 2, 2, 8, 128), jnp.float32),
        in_specs=[
            pl.BlockSpec(memory_space=pltpu.HBM),
            pl.BlockSpec(memory_space=pltpu.SMEM),
            pl.BlockSpec(memory_space=pltpu.HBM),
        ],
        out_specs=vmem,
        scratch_shapes=[
            pltpu.VMEM((4, 16, 256), jnp.int32),
            pltpu.VMEM((4, 16, 256), jnp.float32),
            [pltpu.VMEM((3, 16, 256), kind) for kind in (jnp.int32, jnp.float32)],
            [pltpu.VMEM((7, 8, 256), kind) for kind in (jnp.int32, jnp.float32)],
            pltpu.VMEM((7, 2, 16, 128), jnp.float32),
            pltpu.SemaphoreType.DMA((2,)),
            pltpu.SemaphoreType.DMA((len(MESSAGES), 2)),
            pltpu.SemaphoreType.DMA((len(MESSAGES), 2)),
        ],
        compiler_params=pltpu.CompilerParams(collective_id=0, has_side_effects=True),
        name="exchange",
    )(material, diffusivity, variation)
    return pl.pallas_call(
        stencil_kernel,
        out_shape=jax.ShapeDtypeStruct((27, 2, 8, 128), jnp.float32),
        in_specs=[vmem],
        out_specs=vmem,
        name="stencil",
    )(rho)


def solution(mesh):
    placed = (P("gz", "xy", None), P(), P("gz", "xy", None))
    return jax.shard_map(
        per_device, mesh=mesh, in_specs=placed, out_specs=P(None, "gz", "xy", None), check_vma=False
    )
```

```python
import functools

import jax
import jax.numpy as jnp
from jax import lax
from jax.experimental import pallas as pl
from jax.experimental.pallas import tpu as pltpu
from jax.sharding import PartitionSpec as P

MESH = pl.DeviceIdType.MESH
OUTSIDE = -1e-18
ROW = 16


class Rows:
    def __init__(self, own, edge):
        self.own, self.edge = own, edge

    def __add__(self, other):
        return Rows(self.own + other.own, self.edge + other.edge)

    def __mul__(self, other):
        return Rows(self.own * other.own, self.edge * other.edge)

    def map(self, function):
        return Rows(function(self.own), function(self.edge))


def row_index():
    return lax.broadcasted_iota(jnp.int32, (8, 128), 0)


def lane_index():
    return lax.broadcasted_iota(jnp.int32, (8, 128), 1)


def next_row(value):
    last = row_index() == 7
    own = pltpu.roll(value.own, 7, 0)
    edge = pltpu.roll(value.edge, 7, 0)
    return Rows(jnp.where(last, edge, own), jnp.where(last, own, edge))


def previous_row(value):
    first = row_index() == 0
    return jnp.where(first, pltpu.roll(value.edge, 1, 0), pltpu.roll(value.own, 1, 0))


def next_lane(value):
    return pltpu.roll(value, 127, 1)


def previous_lane(value):
    return pltpu.roll(value, 1, 1)


def next_lane_bounded(value):
    return jnp.where(lane_index() == 127, OUTSIDE, next_lane(value))


def previous_lane_bounded(value):
    return jnp.where(lane_index() == 0, OUTSIDE, previous_lane(value))


def without_last(value):
    return jnp.where(lane_index() == 127, 0.0, value)


def inverse(value):
    return 1.0 / value


class Plane:
    pass


def weights_of(load):
    plane = Plane()
    plane.rho = [[load(xp, yp) for yp in (0, 1)] for xp in (0, 1)]
    plane.low, plane.high, plane.link = [], [], []
    for yp in (0, 1):
        even, odd = plane.rho[0][yp], plane.rho[1][yp]
        before = even + odd
        after = odd + next_row(even)
        link = (before + after).map(inverse)
        plane.low.append(after * link)
        plane.high.append(before * link)
        plane.link.append(link)
    even, odd = plane.rho[0]
    plane.before = even + odd
    plane.after = odd + even.map(next_lane_bounded)
    scale = (plane.before + plane.after).map(inverse)
    plane.y_low = plane.after * scale
    plane.y_high = (plane.before * scale).map(without_last)
    plane.y_low_next = next_row(plane.y_low)
    plane.y_high_next = next_row(plane.y_high)
    return plane


def z_link(lower, upper):
    steps = []
    faces = []
    for yp in (0, 1):
        even = inverse(lower.rho[0][yp].own + upper.rho[0][yp].own)
        odd = (lower.rho[1][yp] + upper.rho[1][yp]).map(inverse)
        low, high = lower.low[yp] * odd, lower.high[yp] * odd
        same = even + (low * upper.low[yp]).own + previous_row(high * upper.high[yp])
        steps.append((same, low * upper.high[yp], high * upper.low[yp]))
        faces.append((even, odd))
    (even_same, even_up, even_down), (odd_same, odd_up, odd_down) = steps
    z = Plane()
    z.faces = faces
    first, second = lower.y_low.own * odd_same, lower.y_high.own * odd_same
    z.same = (
        even_same + first * upper.y_low.own + previous_lane(second * upper.y_high.own),
        first * upper.y_high.own,
        second * upper.y_low.own,
    )
    first, second = lower.y_low * odd_up, lower.y_high * odd_up
    z.up = (
        even_up + first * upper.y_low_next + (second * upper.y_high_next).map(previous_lane),
        first * upper.y_high_next,
        second * upper.y_low_next,
    )
    first, second = lower.y_low_next * odd_down, lower.y_high_next * odd_down
    z.down = (
        even_down + first * upper.y_low + (second * upper.y_high).map(previous_lane),
        first * upper.y_high,
        second * upper.y_low,
    )
    return z


def within(plane, faces_below, faces_above):
    even_before = inverse(plane.before.own)
    even_after = inverse(plane.after.own)
    (odd_e, odd_o) = plane.rho[1]
    odd_before = (odd_e + odd_o).map(inverse)
    odd_after = (odd_o + odd_e.map(next_lane_bounded)).map(inverse)

    def lower_face(face, rho):
        return jnp.where(lane_index() == 0, inverse(rho), previous_lane(face))

    even_lower = lower_face(even_after, plane.rho[0][0].own + OUTSIDE)
    odd_lower = Rows(
        lower_face(odd_after.own, odd_e.own + OUTSIDE),
        lower_face(odd_after.edge, odd_e.edge + OUTSIDE),
    )
    even_sum = [
        even_before + even_lower + faces_below[0][0] + faces_above[0][0],
        even_before + even_after + faces_below[1][0] + faces_above[1][0],
    ]
    odd_sum = [
        odd_before + odd_lower + faces_below[0][1] + faces_above[0][1],
        odd_before + odd_after + faces_below[1][1] + faces_above[1][1],
    ]
    centre, along = [], []
    for yp in (0, 1):
        low, high, link = plane.low[yp], plane.high[yp], plane.link[yp]
        low_sum, high_sum = low * odd_sum[yp], high * odd_sum[yp]
        centre.append(
            even_sum[yp]
            + (link + low_sum * low).own
            + previous_row(link + high_sum * high)
        )
        along.append(
            Rows(
                link.own - low_sum.own * high.own,
                link.edge - low_sum.edge * high.edge,
            )
        )
    even_after = without_last(even_after)
    odd_after = odd_after.map(without_last)
    low_e, low_o = plane.low
    high_e, high_o = plane.high
    low_n, high_n = low_e.map(next_lane), high_e.map(next_lane)
    first, second = low_o * odd_before, high_o * odd_before
    before = (
        even_before + (first * low_e).own + previous_row(second * high_e),
        second * low_e,
        first * high_e,
    )
    first, second = low_o * odd_after, high_o * odd_after
    after = (
        even_after + (first * low_n).own + previous_row(second * high_n),
        first * high_n,
        second * low_n,
    )
    low, high = plane.y_low, plane.y_high
    low_next, high_next = plane.y_low_next, plane.y_high_next
    c = Plane()
    cross = low.own * centre[1]
    c.side = high.own * before[0] + low.own * after[0] - cross * high.own
    c.centre = (
        centre[0]
        + low.own * (cross - before[0] - before[0])
        + previous_lane(high.own * (high.own * centre[1] - after[0] - after[0]))
    )
    one = low * along[1] + before[1]
    two = high * along[1] + after[2]
    c.up = (
        along[0]
        + low_next * one
        + low * before[2]
        + (high_next * two + high * after[1]).map(previous_lane),
        high_next * one + low * after[1],
        low_next * two + high * before[2],
    )
    return c


def z_weights(below, middle, above):
    before = below.rho[0][0] + middle.rho[0][0]
    after = middle.rho[0][0] + above.rho[0][0]
    scale = (before + after).map(inverse)

    def versions(value):
        lane = value.map(next_lane)
        row = next_row(value)
        return (value, lane, row, row.map(next_lane))

    return versions(after * scale), versions(before * scale)


def between(weights, inner, low_link, high_link):
    (lo, lo_j, lo_i, lo_ij), (hi, hi_j, hi_i, hi_ij) = weights

    def term(first, second, low, high, own):
        return second * (low + first * own) + first * high

    same = (
        hi.own * (low_link.same[0] - lo.own * inner.centre) + lo.own * high_link.same[0],
        term(lo.own, hi_j.own, low_link.same[1], high_link.same[1], inner.side),
        term(lo_j.own, hi.own, low_link.same[2], high_link.same[2], inner.side),
    )
    up = (
        term(lo, hi_i, low_link.up[0], high_link.up[0], inner.up[0]),
        term(lo, hi_ij, low_link.up[1], high_link.up[1], inner.up[1]),
        term(lo_j, hi_i, low_link.up[2], high_link.up[2], inner.up[2]),
    )
    down = (
        term(lo_i, hi, low_link.down[0], high_link.down[0], inner.up[0]),
        term(lo_i, hi_j, low_link.down[1], high_link.down[1], inner.up[2]),
        term(lo_ij, hi, low_link.down[2], high_link.down[2], inner.up[1]),
    )
    return same, up, down


def level(own, below, above):
    centre, side = own.centre, own.side
    up = list(own.up)
    (_, hi), inner, link = below
    hi, hi_j, hi_i, hi_ij = hi
    centre = centre + hi.own * (hi.own * inner.centre - link.same[0] - link.same[0])
    side = side + hi.own * (hi_j.own * inner.side + link.same[1]) + hi_j.own * link.same[2]
    up[0] = up[0] + hi * (hi_i * inner.up[0] + link.up[0]) + hi_i * link.down[0]
    up[1] = up[1] + hi * (hi_ij * inner.up[1] + link.up[1]) + hi_ij * link.down[2]
    up[2] = up[2] + hi_j * (hi_i * inner.up[2] + link.up[2]) + hi_i * link.down[1]
    (lo, _), inner, link = above
    lo, lo_j, lo_i, lo_ij = lo
    centre = centre + lo.own * (lo.own * inner.centre - link.same[0] - link.same[0])
    side = side + lo_j.own * (lo.own * inner.side + link.same[1]) + lo.own * link.same[2]
    up[0] = up[0] + lo_i * (lo * inner.up[0] + link.up[0]) + lo * link.down[0]
    up[1] = up[1] + lo_ij * (lo * inner.up[1] + link.up[1]) + lo * link.down[2]
    up[2] = up[2] + lo_i * (lo_j * inner.up[2] + link.up[2]) + lo_j * link.down[1]
    return centre, side, up


def stencil_of(load, store):
    planes = [weights_of(functools.partial(load, p)) for p in range(7)]
    links = [z_link(planes[p], planes[p + 1]) for p in range(6)]
    inner = [None] * 7
    for p in range(1, 6):
        inner[p] = within(planes[p], links[p - 1].faces, links[p].faces)
    weights = [None] * 7
    for p in (1, 3, 5):
        weights[p] = z_weights(planes[p - 1], planes[p], planes[p + 1])
    for p in (1, 3, 5):
        same, up, down = between(weights[p], inner[p], links[p - 1], links[p])
        plane = (p - 1) // 2
        if plane < 2:
            low = functools.partial(store, -1)
            low(0, 0, plane, same[0])
            low(0, 1, plane, same[2])
            low(0, -1, plane, previous_lane(same[1]))
            low(1, 0, plane, down[0].own)
            low(1, 1, plane, down[2].own)
            low(1, -1, plane, previous_lane(down[1].own))
            low(-1, 0, plane, previous_row(up[0]))
            low(-1, 1, plane, previous_row(up[2]))
            low(-1, -1, plane, previous_lane(previous_row(up[1])))
        if plane > 0:
            high = functools.partial(store, 1)
            high(0, 0, plane - 1, same[0])
            high(0, 1, plane - 1, same[1])
            high(0, -1, plane - 1, previous_lane(same[2]))
            high(1, 0, plane - 1, up[0].own)
            high(1, 1, plane - 1, up[1].own)
            high(1, -1, plane - 1, previous_lane(up[2].own))
            high(-1, 0, plane - 1, previous_row(down[0]))
            high(-1, 1, plane - 1, previous_row(down[1]))
            high(-1, -1, plane - 1, previous_lane(previous_row(down[2])))
    for plane in (0, 1):
        p = 2 * plane + 2
        centre, side, up = level(
            inner[p],
            (weights[p - 1], inner[p - 1], links[p - 1]),
            (weights[p + 1], inner[p + 1], links[p]),
        )
        here = functools.partial(store, 0)
        here(0, 0, plane, -centre)
        here(0, 1, plane, side)
        here(0, -1, plane, previous_lane(side))
        here(1, 0, plane, up[0].own)
        here(-1, 0, plane, previous_row(up[0]))
        here(1, 1, plane, up[1].own)
        here(-1, -1, plane, previous_lane(previous_row(up[1])))
        here(1, -1, plane, previous_lane(up[2].own))
        here(-1, 1, plane, previous_row(up[2]))


def split_lanes(value):
    lane = lax.broadcasted_iota(jnp.int32, (value.shape[0], 128), 1)
    left, right = value[:, :128], value[:, 128:]
    first = (lane * 2) % 128 + lane // 64
    left = jnp.take_along_axis(left, first, axis=1)
    right = jnp.take_along_axis(right, (first + 1) % 2 + first // 2 * 2, axis=1)
    even = jnp.where(lane < 64, left, right)
    odd = pltpu.roll(jnp.where(lane < 64, right, left), 64, 1)
    return even, odd


SENT = {-1: (0, 1), 0: (0, 4), 1: (2, 2)}
LANDED = {-1: 6, 0: 2, 1: 0}
AHEAD = [(0, 1), (-1, 1), (1, 1)]
SIDE = [(-1, 0), (1, 0)]
BACK = [(0, -1), (-1, -1), (1, -1)]
MESSAGES = AHEAD + SIDE + BACK


def exchange_kernel(
    material, diffusivity, variation, out, blocks, facts, borders, edges, split, load_sem, send_sem, recv_sem, here
):
    gz, xy = lax.axis_index("gz"), lax.axis_index("xy")
    count_z, count_x = lax.axis_size("gz"), lax.axis_size("xy")
    inputs = (material, variation)
    own = (blocks, facts)

    def exists(dz, dx):
        inside = None
        for at, step, count in ((gz, dz, count_z), (xy, dx, count_x)):
            if step:
                good = at + step < count if step > 0 else at > 0
                inside = good if inside is None else jnp.logical_and(inside, good)
        return inside

    def device(dz, dx):
        return {"gz": gz + dz, "xy": xy + dx}

    def copies(dz, dx):
        n = MESSAGES.index((dz, dx))
        first, planes = SENT[dz]
        made = []
        for which in (0, 1):
            source = inputs[which].at[pl.ds(first, planes)]
            if dx == 0:
                target = borders[which].at[pl.ds(0 if dz > 0 else 2, planes)]
            else:
                row, rows, at = (14, 2, 6) if dx > 0 else (0, 1, 0)
                source = inputs[which].at[pl.ds(first, planes), pl.ds(row, rows)]
                target = edges[which].at[pl.ds(LANDED[dz], planes), pl.ds(at, rows)]
            made.append(
                pltpu.make_async_remote_copy(
                    src_ref=source,
                    dst_ref=target,
                    send_sem=send_sem.at[n, which],
                    recv_sem=recv_sem.at[n, which],
                    device_id=device(dz, dx),
                    device_id_type=MESH,
                )
            )
        return made

    def send(dz, dx, condition=None):
        good = exists(dz, dx)

        @pl.when(good if condition is None else jnp.logical_and(good, condition))
        def _():
            for copy in copies(dz, dx):
                copy.start()

    def receive(dz, dx):
        @pl.when(exists(-dz, -dx))
        def _():
            for copy in copies(dz, dx):
                copy.wait_recv()

    barrier = pltpu.get_barrier_semaphore()
    place_in_row = lax.rem(xy, ROW)
    first = jnp.logical_and(place_in_row == 0, xy > 0)
    last = jnp.logical_and(place_in_row == ROW - 1, xy < count_x - 1)
    inner = jnp.logical_not(jnp.logical_or(first, last))
    not_last = jnp.logical_not(last)
    before_last = lax.rem(xy + 1, ROW) == ROW - 1
    before_last = jnp.logical_and(before_last, xy < count_x - 2)

    def greet(semaphore, dz, dx, condition=None):
        good = exists(dz, dx)

        @pl.when(good if condition is None else jnp.logical_and(good, condition))
        def _():
            pl.semaphore_signal(
                semaphore, inc=1, device_id=device(dz, dx), device_id_type=MESH
            )

    for dz, dx in BACK:
        greet(barrier, dz, dx)
    for dz, dx in SIDE:
        greet(barrier, dz, dx, not_last)
    for dz, dx in AHEAD:
        greet(barrier, dz, dx, jnp.logical_not(jnp.logical_or(last, before_last)))
    loads = [pltpu.make_async_copy(inputs[n], own[n], load_sem.at[n]) for n in (0, 1)]
    for copy in loads:
        copy.start()
    one = jnp.int32(1)
    z_sides = jnp.where(gz > 0, one, 0) + jnp.where(gz < count_z - 1, one, 0)
    expected = (
        jnp.where(xy < count_x - 1, z_sides + 1, 0)
        + jnp.where(last, 0, z_sides)
        + jnp.where(jnp.logical_and(inner, xy > 0), z_sides + 1, 0)
    )
    pl.semaphore_wait(barrier, expected)
    for dz, dx in AHEAD:
        greet(here, dz, dx, last)
    for dz, dx in AHEAD:
        send(dz, dx)
    for dz, dx in SIDE:
        send(dz, dx, not_last)
    for dz, dx in BACK:
        send(dz, dx, inner)

    table = [diffusivity[which] for which in range(8)]

    def resistivity(which, factor):
        values = table
        for bit in (1, 2, 4):
            chosen = (which & bit) != 0
            values = [
                jnp.where(chosen, values[2 * n + 1], values[2 * n])
                for n in range(len(values) // 2)
            ]
        return -0.5 / (values[0] * factor)

    def place(plane, which, factor):
        for yp, half in enumerate(split_lanes(resistivity(which, factor))):
            split[plane, yp] = half
            for xp in (0, 1):
                out[0, plane, xp, yp] = split[plane, yp, pl.ds(xp, 8, stride=2), :]

    for copy in loads:
        copy.wait()
    for k in range(4):
        place(k + 2, blocks[k], facts[k])

    @pl.when(last)
    def _():
        for dz, dx in AHEAD:
            receive(dz, dx)
        for dz, dx in BACK:
            send(dz, dx)
        for dz, dx in SIDE:
            send(dz, dx)

    for dz, dx in SIDE:
        receive(dz, dx)
    for n, plane in enumerate((0, 1, 6)):
        place(plane, borders[0][n], borders[1][n])
    for dz, dx in BACK:
        receive(dz, dx)

    @pl.when(first)
    def _():
        pl.semaphore_wait(here, z_sides + 1)
        for dz, dx in BACK:
            send(dz, dx)

    @pl.when(not_last)
    def _():
        for dz, dx in AHEAD:
            receive(dz, dx)

    bottom = row_index() == 7
    for plane in range(7):
        halves = split_lanes(resistivity(edges[0][plane], edges[1][plane]))
        for yp, half in enumerate(halves):
            out[1, plane, 0, yp] = jnp.where(bottom, pltpu.roll(half, 1, 0), half)
            out[1, plane, 1, yp] = half
    for dz, dx in MESSAGES:
        @pl.when(exists(dz, dx))
        def _():
            for copy in copies(dz, dx):
                copy.wait_send()

    @pl.when(gz == 0)
    def _():
        out[:, 0:2] = jnp.full((2, 2, 2, 2, 8, 128), OUTSIDE, jnp.float32)

    @pl.when(gz == count_z - 1)
    def _():
        out[:, 6] = jnp.full((2, 2, 2, 8, 128), OUTSIDE, jnp.float32)

    @pl.when(xy == 0)
    def _():
        out[1, :, :, :, 7, :] = jnp.full((7, 2, 2, 128), OUTSIDE, jnp.float32)

    @pl.when(xy == count_x - 1)
    def _():
        out[1, :, 0, :, 0, :] = jnp.full((7, 2, 128), OUTSIDE, jnp.float32)


def stencil_kernel(rho, out):
    gz, xy = lax.axis_index("gz"), lax.axis_index("xy")

    def load(p, xp, yp):
        return Rows(rho[0, p, xp, yp], rho[1, p, xp, yp])

    def store(dz, dx, dy, plane, value):
        out[9 * (dz + 1) + 3 * (dx + 1) + dy + 1, plane] = value

    stencil_of(load, store)
    nothing = jnp.zeros((1, 128), jnp.float32)

    def clear_row(dx, row):
        for dz in (-1, 0, 1):
            for dy in (-1, 0, 1):
                for plane in (0, 1):
                    entry = 9 * (dz + 1) + 3 * (dx + 1) + dy + 1
                    out[entry, plane, pl.ds(row, 1), :] = nothing

    @pl.when(xy == 0)
    def _():
        clear_row(-1, 0)

    @pl.when(xy == lax.axis_size("xy") - 1)
    def _():
        clear_row(1, 7)

    @pl.when(gz == 0)
    def _():
        out[0:9, 0] = jnp.zeros((9, 8, 128), jnp.float32)

    @pl.when(gz == lax.axis_size("gz") - 1)
    def _():
        out[18:27, 1] = jnp.zeros((9, 8, 128), jnp.float32)


def per_device(material, diffusivity, variation):
    vmem = pl.BlockSpec(memory_space=pltpu.VMEM)
    rho = pl.pallas_call(
        exchange_kernel,
        out_shape=jax.ShapeDtypeStruct((2, 7, 2, 2, 8, 128), jnp.float32),
        in_specs=[
            pl.BlockSpec(memory_space=pltpu.HBM),
            pl.BlockSpec(memory_space=pltpu.SMEM),
            pl.BlockSpec(memory_space=pltpu.HBM),
        ],
        out_specs=vmem,
        scratch_shapes=[
            pltpu.VMEM((4, 16, 256), jnp.int32),
            pltpu.VMEM((4, 16, 256), jnp.float32),
            [pltpu.VMEM((3, 16, 256), kind) for kind in (jnp.int32, jnp.float32)],
            [pltpu.VMEM((7, 8, 256), kind) for kind in (jnp.int32, jnp.float32)],
            pltpu.VMEM((7, 2, 16, 128), jnp.float32),
            pltpu.SemaphoreType.DMA((2,)),
            pltpu.SemaphoreType.DMA((len(MESSAGES), 2)),
            pltpu.SemaphoreType.DMA((len(MESSAGES), 2)),
            pltpu.SemaphoreType.REGULAR,
        ],
        compiler_params=pltpu.CompilerParams(collective_id=0, has_side_effects=True),
        name="exchange",
    )(material, diffusivity, variation)
    return pl.pallas_call(
        stencil_kernel,
        out_shape=jax.ShapeDtypeStruct((27, 2, 8, 128), jnp.float32),
        in_specs=[vmem],
        out_specs=vmem,
        name="stencil",
    )(rho)


def solution(mesh):
    placed = (P("gz", "xy", None), P(), P("gz", "xy", None))
    return jax.shard_map(
        per_device, mesh=mesh, in_specs=placed, out_specs=P(None, "gz", "xy", None), check_vma=False
    )
```

```python
import functools

import jax
import jax.numpy as jnp
from jax import lax
from jax.experimental import pallas as pl
from jax.experimental.pallas import tpu as pltpu
from jax.sharding import PartitionSpec as P

MESH = pl.DeviceIdType.MESH
OUTSIDE = -1e-18
ROW = 16
VMEM_BYTES = 4 << 20


class Rows:
    def __init__(self, own, edge):
        self.own, self.edge = own, edge

    def __add__(self, other):
        return Rows(self.own + other.own, self.edge + other.edge)

    def __mul__(self, other):
        return Rows(self.own * other.own, self.edge * other.edge)

    def map(self, function):
        return Rows(function(self.own), function(self.edge))


def row_index():
    return lax.broadcasted_iota(jnp.int32, (8, 128), 0)


def lane_index():
    return lax.broadcasted_iota(jnp.int32, (8, 128), 1)


def next_row(value):
    last = row_index() == 7
    own = pltpu.roll(value.own, 7, 0)
    edge = pltpu.roll(value.edge, 7, 0)
    return Rows(jnp.where(last, edge, own), jnp.where(last, own, edge))


def previous_row(value):
    first = row_index() == 0
    return jnp.where(first, pltpu.roll(value.edge, 1, 0), pltpu.roll(value.own, 1, 0))


def next_lane(value):
    return pltpu.roll(value, 127, 1)


def previous_lane(value):
    return pltpu.roll(value, 1, 1)


def next_lane_bounded(value):
    return jnp.where(lane_index() == 127, OUTSIDE, next_lane(value))


def previous_lane_bounded(value):
    return jnp.where(lane_index() == 0, OUTSIDE, previous_lane(value))


def without_last(value):
    return jnp.where(lane_index() == 127, 0.0, value)


def inverse(value):
    return 1.0 / value


class Plane:
    pass


def weights_of(load):
    plane = Plane()
    plane.rho = [[load(xp, yp) for yp in (0, 1)] for xp in (0, 1)]
    plane.low, plane.high, plane.link = [], [], []
    for yp in (0, 1):
        even, odd = plane.rho[0][yp], plane.rho[1][yp]
        before = even + odd
        after = odd + next_row(even)
        link = (before + after).map(inverse)
        plane.low.append(after * link)
        plane.high.append(before * link)
        plane.link.append(link)
    even, odd = plane.rho[0]
    plane.before = even + odd
    plane.after = odd + even.map(next_lane_bounded)
    scale = (plane.before + plane.after).map(inverse)
    plane.y_low = plane.after * scale
    plane.y_high = (plane.before * scale).map(without_last)
    plane.y_low_next = next_row(plane.y_low)
    plane.y_high_next = next_row(plane.y_high)
    return plane


def z_link(lower, upper):
    steps = []
    faces = []
    for yp in (0, 1):
        even = inverse(lower.rho[0][yp].own + upper.rho[0][yp].own)
        odd = (lower.rho[1][yp] + upper.rho[1][yp]).map(inverse)
        low, high = lower.low[yp] * odd, lower.high[yp] * odd
        same = even + (low * upper.low[yp]).own + previous_row(high * upper.high[yp])
        steps.append((same, low * upper.high[yp], high * upper.low[yp]))
        faces.append((even, odd))
    (even_same, even_up, even_down), (odd_same, odd_up, odd_down) = steps
    z = Plane()
    z.faces = faces
    first, second = lower.y_low.own * odd_same, lower.y_high.own * odd_same
    z.same = (
        even_same + first * upper.y_low.own + previous_lane(second * upper.y_high.own),
        first * upper.y_high.own,
        second * upper.y_low.own,
    )
    first, second = lower.y_low * odd_up, lower.y_high * odd_up
    z.up = (
        even_up + first * upper.y_low_next + (second * upper.y_high_next).map(previous_lane),
        first * upper.y_high_next,
        second * upper.y_low_next,
    )
    first, second = lower.y_low_next * odd_down, lower.y_high_next * odd_down
    z.down = (
        even_down + first * upper.y_low + (second * upper.y_high).map(previous_lane),
        first * upper.y_high,
        second * upper.y_low,
    )
    return z


def within(plane, faces_below, faces_above):
    even_before = inverse(plane.before.own)
    even_after = inverse(plane.after.own)
    (odd_e, odd_o) = plane.rho[1]
    odd_before = (odd_e + odd_o).map(inverse)
    odd_after = (odd_o + odd_e.map(next_lane_bounded)).map(inverse)

    def lower_face(face, rho):
        return jnp.where(lane_index() == 0, inverse(rho), previous_lane(face))

    even_lower = lower_face(even_after, plane.rho[0][0].own + OUTSIDE)
    odd_lower = Rows(
        lower_face(odd_after.own, odd_e.own + OUTSIDE),
        lower_face(odd_after.edge, odd_e.edge + OUTSIDE),
    )
    even_sum = [
        even_before + even_lower + faces_below[0][0] + faces_above[0][0],
        even_before + even_after + faces_below[1][0] + faces_above[1][0],
    ]
    odd_sum = [
        odd_before + odd_lower + faces_below[0][1] + faces_above[0][1],
        odd_before + odd_after + faces_below[1][1] + faces_above[1][1],
    ]
    centre, along = [], []
    for yp in (0, 1):
        low, high, link = plane.low[yp], plane.high[yp], plane.link[yp]
        low_sum, high_sum = low * odd_sum[yp], high * odd_sum[yp]
        centre.append(
            even_sum[yp]
            + (link + low_sum * low).own
            + previous_row(link + high_sum * high)
        )
        along.append(
            Rows(
                link.own - low_sum.own * high.own,
                link.edge - low_sum.edge * high.edge,
            )
        )
    even_after = without_last(even_after)
    odd_after = odd_after.map(without_last)
    low_e, low_o = plane.low
    high_e, high_o = plane.high
    low_n, high_n = low_e.map(next_lane), high_e.map(next_lane)
    first, second = low_o * odd_before, high_o * odd_before
    before = (
        even_before + (first * low_e).own + previous_row(second * high_e),
        second * low_e,
        first * high_e,
    )
    first, second = low_o * odd_after, high_o * odd_after
    after = (
        even_after + (first * low_n).own + previous_row(second * high_n),
        first * high_n,
        second * low_n,
    )
    low, high = plane.y_low, plane.y_high
    low_next, high_next = plane.y_low_next, plane.y_high_next
    c = Plane()
    cross = low.own * centre[1]
    c.side = high.own * before[0] + low.own * after[0] - cross * high.own
    c.centre = (
        centre[0]
        + low.own * (cross - before[0] - before[0])
        + previous_lane(high.own * (high.own * centre[1] - after[0] - after[0]))
    )
    one = low * along[1] + before[1]
    two = high * along[1] + after[2]
    c.up = (
        along[0]
        + low_next * one
        + low * before[2]
        + (high_next * two + high * after[1]).map(previous_lane),
        high_next * one + low * after[1],
        low_next * two + high * before[2],
    )
    return c


def z_weights(below, middle, above):
    before = below.rho[0][0] + middle.rho[0][0]
    after = middle.rho[0][0] + above.rho[0][0]
    scale = (before + after).map(inverse)

    def versions(value):
        lane = value.map(next_lane)
        row = next_row(value)
        return (value, lane, row, row.map(next_lane))

    return versions(after * scale), versions(before * scale)


def between(weights, inner, low_link, high_link):
    (lo, lo_j, lo_i, lo_ij), (hi, hi_j, hi_i, hi_ij) = weights

    def term(first, second, low, high, own):
        return second * (low + first * own) + first * high

    same = (
        hi.own * (low_link.same[0] - lo.own * inner.centre) + lo.own * high_link.same[0],
        term(lo.own, hi_j.own, low_link.same[1], high_link.same[1], inner.side),
        term(lo_j.own, hi.own, low_link.same[2], high_link.same[2], inner.side),
    )
    up = (
        term(lo, hi_i, low_link.up[0], high_link.up[0], inner.up[0]),
        term(lo, hi_ij, low_link.up[1], high_link.up[1], inner.up[1]),
        term(lo_j, hi_i, low_link.up[2], high_link.up[2], inner.up[2]),
    )
    down = (
        term(lo_i, hi, low_link.down[0], high_link.down[0], inner.up[0]),
        term(lo_i, hi_j, low_link.down[1], high_link.down[1], inner.up[2]),
        term(lo_ij, hi, low_link.down[2], high_link.down[2], inner.up[1]),
    )
    return same, up, down


def level(own, below, above):
    centre, side = own.centre, own.side
    up = list(own.up)
    (_, hi), inner, link = below
    hi, hi_j, hi_i, hi_ij = hi
    centre = centre + hi.own * (hi.own * inner.centre - link.same[0] - link.same[0])
    side = side + hi.own * (hi_j.own * inner.side + link.same[1]) + hi_j.own * link.same[2]
    up[0] = up[0] + hi * (hi_i * inner.up[0] + link.up[0]) + hi_i * link.down[0]
    up[1] = up[1] + hi * (hi_ij * inner.up[1] + link.up[1]) + hi_ij * link.down[2]
    up[2] = up[2] + hi_j * (hi_i * inner.up[2] + link.up[2]) + hi_i * link.down[1]
    (lo, _), inner, link = above
    lo, lo_j, lo_i, lo_ij = lo
    centre = centre + lo.own * (lo.own * inner.centre - link.same[0] - link.same[0])
    side = side + lo_j.own * (lo.own * inner.side + link.same[1]) + lo.own * link.same[2]
    up[0] = up[0] + lo_i * (lo * inner.up[0] + link.up[0]) + lo * link.down[0]
    up[1] = up[1] + lo_ij * (lo * inner.up[1] + link.up[1]) + lo * link.down[2]
    up[2] = up[2] + lo_i * (lo_j * inner.up[2] + link.up[2]) + lo_j * link.down[1]
    return centre, side, up


def stencil_of(load, store):
    planes = [weights_of(functools.partial(load, p)) for p in range(7)]
    links = [z_link(planes[p], planes[p + 1]) for p in range(6)]
    inner = [None] * 7
    for p in range(1, 6):
        inner[p] = within(planes[p], links[p - 1].faces, links[p].faces)
    weights = [None] * 7
    for p in (1, 3, 5):
        weights[p] = z_weights(planes[p - 1], planes[p], planes[p + 1])
    for p in (1, 3, 5):
        same, up, down = between(weights[p], inner[p], links[p - 1], links[p])
        plane = (p - 1) // 2
        if plane < 2:
            low = functools.partial(store, -1)
            low(0, 0, plane, same[0])
            low(0, 1, plane, same[2])
            low(0, -1, plane, previous_lane(same[1]))
            low(1, 0, plane, down[0].own)
            low(1, 1, plane, down[2].own)
            low(1, -1, plane, previous_lane(down[1].own))
            low(-1, 0, plane, previous_row(up[0]))
            low(-1, 1, plane, previous_row(up[2]))
            low(-1, -1, plane, previous_lane(previous_row(up[1])))
        if plane > 0:
            high = functools.partial(store, 1)
            high(0, 0, plane - 1, same[0])
            high(0, 1, plane - 1, same[1])
            high(0, -1, plane - 1, previous_lane(same[2]))
            high(1, 0, plane - 1, up[0].own)
            high(1, 1, plane - 1, up[1].own)
            high(1, -1, plane - 1, previous_lane(up[2].own))
            high(-1, 0, plane - 1, previous_row(down[0]))
            high(-1, 1, plane - 1, previous_row(down[1]))
            high(-1, -1, plane - 1, previous_lane(previous_row(down[2])))
    for plane in (0, 1):
        p = 2 * plane + 2
        centre, side, up = level(
            inner[p],
            (weights[p - 1], inner[p - 1], links[p - 1]),
            (weights[p + 1], inner[p + 1], links[p]),
        )
        here = functools.partial(store, 0)
        here(0, 0, plane, -centre)
        here(0, 1, plane, side)
        here(0, -1, plane, previous_lane(side))
        here(1, 0, plane, up[0].own)
        here(-1, 0, plane, previous_row(up[0]))
        here(1, 1, plane, up[1].own)
        here(-1, -1, plane, previous_lane(previous_row(up[1])))
        here(1, -1, plane, previous_lane(up[2].own))
        here(-1, 1, plane, previous_row(up[2]))


def split_lanes(value):
    lane = lax.broadcasted_iota(jnp.int32, (value.shape[0], 128), 1)
    left, right = value[:, :128], value[:, 128:]
    first = (lane * 2) % 128 + lane // 64
    left = jnp.take_along_axis(left, first, axis=1)
    right = jnp.take_along_axis(right, (first + 1) % 2 + first // 2 * 2, axis=1)
    even = jnp.where(lane < 64, left, right)
    odd = pltpu.roll(jnp.where(lane < 64, right, left), 64, 1)
    return even, odd


SENT = {-1: (0, 1), 0: (0, 4), 1: (2, 2)}
LANDED = {-1: 6, 0: 2, 1: 0}
AHEAD = [(-1, 1), (1, 1), (0, 1)]
SIDE = [(-1, 0), (1, 0)]
BACK = [(0, -1), (-1, -1), (1, -1)]
MESSAGES = AHEAD + SIDE + BACK


def exchange_kernel(
    material, diffusivity, variation, out, blocks, facts, levels, borders, edges, split, load_sem, send_sem, recv_sem, here
):
    gz, xy = lax.axis_index("gz"), lax.axis_index("xy")
    count_z, count_x = lax.axis_size("gz"), lax.axis_size("xy")
    inputs = (material, variation)

    def exists(dz, dx):
        inside = None
        for at, step, count in ((gz, dz, count_z), (xy, dx, count_x)):
            if step:
                good = at + step < count if step > 0 else at > 0
                inside = good if inside is None else jnp.logical_and(inside, good)
        return inside

    def device(dz, dx):
        return {"gz": gz + dz, "xy": xy + dx}

    def copies(dz, dx):
        n = MESSAGES.index((dz, dx))
        first, planes = SENT[dz]
        made = []
        for which in (0, 1):
            source = inputs[which].at[pl.ds(first, planes)]
            if dx == 0:
                target = borders[which].at[pl.ds(0 if dz > 0 else 2, planes)]
            else:
                row, rows, at = (14, 2, 6) if dx > 0 else (0, 1, 0)
                source = inputs[which].at[pl.ds(first, planes), pl.ds(row, rows)]
                target = edges[which].at[pl.ds(LANDED[dz], planes), pl.ds(at, rows)]
            made.append(
                pltpu.make_async_remote_copy(
                    src_ref=source,
                    dst_ref=target,
                    send_sem=send_sem.at[n, which],
                    recv_sem=recv_sem.at[n, which],
                    device_id=device(dz, dx),
                    device_id_type=MESH,
                )
            )
        return made

    def send(dz, dx, condition=None):
        good = exists(dz, dx)

        @pl.when(good if condition is None else jnp.logical_and(good, condition))
        def _():
            for copy in copies(dz, dx):
                copy.start()

    def receive(dz, dx):
        @pl.when(exists(-dz, -dx))
        def _():
            for copy in copies(dz, dx):
                copy.wait_recv()

    barrier = pltpu.get_barrier_semaphore()
    place_in_row = lax.rem(xy, ROW)
    first = jnp.logical_and(place_in_row == 0, xy > 0)
    last = jnp.logical_and(place_in_row == ROW - 1, xy < count_x - 1)
    inner = jnp.logical_not(jnp.logical_or(first, last))
    not_last = jnp.logical_not(last)
    before_last = lax.rem(xy + 1, ROW) == ROW - 1
    before_last = jnp.logical_and(before_last, xy < count_x - 2)

    def greet(semaphore, dz, dx, condition=None):
        good = exists(dz, dx)

        @pl.when(good if condition is None else jnp.logical_and(good, condition))
        def _():
            pl.semaphore_signal(
                semaphore, inc=1, device_id=device(dz, dx), device_id_type=MESH
            )

    for dz, dx in BACK:
        greet(barrier, dz, dx)
    for dz, dx in SIDE:
        greet(barrier, dz, dx, not_last)
    for dz, dx in AHEAD:
        greet(barrier, dz, dx, jnp.logical_not(jnp.logical_or(last, before_last)))
    loads = [
        pltpu.make_async_copy(source, target, load_sem.at[n])
        for n, (source, target) in enumerate(
            ((material, blocks), (variation, facts), (diffusivity, levels))
        )
    ]
    for copy in loads:
        copy.start()
    one = jnp.int32(1)
    z_sides = jnp.where(gz > 0, one, 0) + jnp.where(gz < count_z - 1, one, 0)
    expected = (
        jnp.where(xy < count_x - 1, z_sides + 1, 0)
        + jnp.where(last, 0, z_sides)
        + jnp.where(jnp.logical_and(inner, xy > 0), z_sides + 1, 0)
    )
    pl.semaphore_wait(barrier, expected)
    for dz, dx in AHEAD:
        greet(here, dz, dx, last)
    for dz, dx in AHEAD:
        send(dz, dx)
    for dz, dx in SIDE:
        send(dz, dx, not_last)
    for dz, dx in BACK:
        send(dz, dx, inner)

    def resistivity(which, factor):
        values = table
        for bit in (1, 2, 4):
            chosen = (which & bit) != 0
            values = [
                jnp.where(chosen, values[2 * n + 1], values[2 * n])
                for n in range(len(values) // 2)
            ]
        return -0.5 / (values[0] * factor)

    def place(plane, which, factor):
        for yp, half in enumerate(split_lanes(resistivity(which, factor))):
            split[plane, yp] = half
            for xp in (0, 1):
                out[0, plane, xp, yp] = split[plane, yp, pl.ds(xp, 8, stride=2), :]

    for copy in loads:
        copy.wait()
    table = [levels[which] for which in range(8)]
    for k in range(4):
        place(k + 2, blocks[k], facts[k])

    @pl.when(last)
    def _():
        for dz, dx in AHEAD:
            receive(dz, dx)
        for dz, dx in BACK:
            send(dz, dx)
        for dz, dx in SIDE:
            send(dz, dx)

    for dz, dx in SIDE:
        receive(dz, dx)
    for n, plane in enumerate((0, 1, 6)):
        place(plane, borders[0][n], borders[1][n])
    for dz, dx in BACK:
        receive(dz, dx)

    @pl.when(first)
    def _():
        pl.semaphore_wait(here, z_sides + 1)
        for dz, dx in BACK:
            send(dz, dx)

    @pl.when(not_last)
    def _():
        for dz, dx in AHEAD:
            receive(dz, dx)

    bottom = row_index() == 7
    for plane in range(7):
        halves = split_lanes(resistivity(edges[0][plane], edges[1][plane]))
        for yp, half in enumerate(halves):
            out[1, plane, 0, yp] = jnp.where(bottom, pltpu.roll(half, 1, 0), half)
            out[1, plane, 1, yp] = half
    for dz, dx in MESSAGES:
        @pl.when(exists(dz, dx))
        def _():
            for copy in copies(dz, dx):
                copy.wait_send()

    @pl.when(gz == 0)
    def _():
        out[:, 0:2] = jnp.full((2, 2, 2, 2, 8, 128), OUTSIDE, jnp.float32)

    @pl.when(gz == count_z - 1)
    def _():
        out[:, 6] = jnp.full((2, 2, 2, 8, 128), OUTSIDE, jnp.float32)

    @pl.when(xy == 0)
    def _():
        out[1, :, :, :, 7, :] = jnp.full((7, 2, 2, 128), OUTSIDE, jnp.float32)

    @pl.when(xy == count_x - 1)
    def _():
        out[1, :, 0, :, 0, :] = jnp.full((7, 2, 128), OUTSIDE, jnp.float32)


def stencil_kernel(rho, out):
    gz, xy = lax.axis_index("gz"), lax.axis_index("xy")

    def load(p, xp, yp):
        return Rows(rho[0, p, xp, yp], rho[1, p, xp, yp])

    def store(dz, dx, dy, plane, value):
        out[9 * (dz + 1) + 3 * (dx + 1) + dy + 1, plane] = value

    stencil_of(load, store)
    nothing = jnp.zeros((1, 128), jnp.float32)

    def clear_row(dx, row):
        for dz in (-1, 0, 1):
            for dy in (-1, 0, 1):
                for plane in (0, 1):
                    entry = 9 * (dz + 1) + 3 * (dx + 1) + dy + 1
                    out[entry, plane, pl.ds(row, 1), :] = nothing

    @pl.when(xy == 0)
    def _():
        clear_row(-1, 0)

    @pl.when(xy == lax.axis_size("xy") - 1)
    def _():
        clear_row(1, 7)

    @pl.when(gz == 0)
    def _():
        out[0:9, 0] = jnp.zeros((9, 8, 128), jnp.float32)

    @pl.when(gz == lax.axis_size("gz") - 1)
    def _():
        out[18:27, 1] = jnp.zeros((9, 8, 128), jnp.float32)


def per_device(material, diffusivity, variation):
    vmem = pl.BlockSpec(memory_space=pltpu.VMEM)
    material, diffusivity, variation = (
        pltpu.with_memory_space_constraint(x, pltpu.HBM)
        for x in (material, diffusivity, variation)
    )
    rho = pl.pallas_call(
        exchange_kernel,
        out_shape=jax.ShapeDtypeStruct((2, 7, 2, 2, 8, 128), jnp.float32),
        in_specs=[
            pl.BlockSpec(memory_space=pltpu.HBM),
            pl.BlockSpec(memory_space=pltpu.HBM),
            pl.BlockSpec(memory_space=pltpu.HBM),
        ],
        out_specs=vmem,
        scratch_shapes=[
            pltpu.VMEM((4, 16, 256), jnp.int32),
            pltpu.VMEM((4, 16, 256), jnp.float32),
            pltpu.SMEM((8,), jnp.float32),
            [pltpu.VMEM((3, 16, 256), kind) for kind in (jnp.int32, jnp.float32)],
            [pltpu.VMEM((7, 8, 256), kind) for kind in (jnp.int32, jnp.float32)],
            pltpu.VMEM((7, 2, 16, 128), jnp.float32),
            pltpu.SemaphoreType.DMA((3,)),
            pltpu.SemaphoreType.DMA((len(MESSAGES), 2)),
            pltpu.SemaphoreType.DMA((len(MESSAGES), 2)),
            pltpu.SemaphoreType.REGULAR,
        ],
        compiler_params=pltpu.CompilerParams(
            collective_id=0, has_side_effects=True, vmem_limit_bytes=VMEM_BYTES
        ),
        name="exchange",
    )(material, diffusivity, variation)
    return pl.pallas_call(
        stencil_kernel,
        out_shape=jax.ShapeDtypeStruct((27, 2, 8, 128), jnp.float32),
        in_specs=[vmem],
        out_specs=vmem,
        compiler_params=pltpu.CompilerParams(vmem_limit_bytes=VMEM_BYTES),
        name="stencil",
    )(rho)


def solution(mesh):
    placed = (P("gz", "xy", None), P(), P("gz", "xy", None))
    return jax.shard_map(
        per_device, mesh=mesh, in_specs=placed, out_specs=P(None, "gz", "xy", None), check_vma=False
    )
```

```python
import functools

import jax
import jax.numpy as jnp
from jax import lax
from jax.experimental import pallas as pl
from jax.experimental.pallas import tpu as pltpu
from jax.sharding import PartitionSpec as P

MESH = pl.DeviceIdType.MESH
OUTSIDE = -1e-18
ROW = 16
VMEM_BYTES = 4 << 20


def row_index():
    return lax.broadcasted_iota(jnp.int32, (8, 128), 0)


def lane_index():
    return lax.broadcasted_iota(jnp.int32, (8, 128), 1)


def previous_row(value):
    return jnp.where(row_index() == 0, 0.0, pltpu.roll(value, 1, 0))


def next_lane(value):
    return pltpu.roll(value, 127, 1)


def previous_lane(value):
    return pltpu.roll(value, 1, 1)


def next_lane_bounded(value):
    return jnp.where(lane_index() == 127, OUTSIDE, next_lane(value))


def without_last(value):
    return jnp.where(lane_index() == 127, 0.0, value)


def inverse(value):
    return 1.0 / value


class Group:
    def __init__(self, **arrays):
        self.__dict__.update(arrays)

    def moved(self, step):
        def roll(value):
            if isinstance(value, (tuple, list)):
                return tuple(roll(part) for part in value)
            return value if value is None else pltpu.roll(value, -step % 8, 0)

        return Group(**{name: roll(value) for name, value in self.__dict__.items()})


def x_weights(even, odd, even_next):
    low, high, link = [], [], []
    for yp in (0, 1):
        before = even[yp] + odd[yp]
        after = odd[yp] + even_next[yp]
        scale = inverse(before + after)
        low.append(after * scale)
        high.append(before * scale)
        link.append(scale)
    return {"low": low, "high": high, "link": link, "odd": odd, "even": even}


def y_weights(even):
    before = even[0] + even[1]
    after = even[1] + next_lane_bounded(even[0])
    scale = inverse(before + after)
    return after * scale, without_last(before * scale), before, after


def z_link(lower, upper, edge):
    steps = []
    faces = []
    for yp in (0, 1):
        odd = inverse(lower.odd[yp] + upper.odd[yp])
        low, high = lower.low[yp] * odd, lower.high[yp] * odd
        same = high * upper.high[yp]
        even = None
        if not edge:
            even = inverse(lower.even[yp] + upper.even[yp])
            same = even + low * upper.low[yp] + previous_row(same)
        steps.append((same, low * upper.high[yp], high * upper.low[yp]))
        faces.append((even, odd))
    (even_same, even_up, even_down), (odd_same, odd_up, odd_down) = steps

    def y_step(even, odd, lower_y, upper_y):
        first, second = lower_y[0] * odd, lower_y[1] * odd
        return (
            even + first * upper_y[0] + previous_lane(second * upper_y[1]),
            first * upper_y[1],
            second * upper_y[0],
        )

    return Group(
        faces=tuple(faces),
        same=y_step(even_same, odd_same, lower.y_same, upper.y_same),
        up=y_step(even_up, odd_up, lower.y, upper.y_next),
        down=y_step(even_down, odd_down, lower.y_next, upper.y),
    )


def within(plane, faces_below, faces_above, edge):
    odd_e, odd_o = plane.odd

    def lower_face(face, rho):
        return jnp.where(lane_index() == 0, inverse(rho + OUTSIDE), previous_lane(face))

    odd_before = inverse(odd_e + odd_o)
    odd_after = inverse(odd_o + next_lane_bounded(odd_e))
    odd_sum = [
        odd_before + lower_face(odd_after, odd_e) + faces_below[0][1] + faces_above[0][1],
        odd_before + odd_after + faces_below[1][1] + faces_above[1][1],
    ]
    odd_after = without_last(odd_after)
    if not edge:
        even_before, even_after = inverse(plane.before), inverse(plane.after)
        even_lower = lower_face(even_after, plane.even[0])
        even_sum = [
            even_before + even_lower + faces_below[0][0] + faces_above[0][0],
            even_before + even_after + faces_below[1][0] + faces_above[1][0],
        ]
        even_after = without_last(even_after)
    centre, along = [], []
    for yp in (0, 1):
        low, high, link = plane.low[yp], plane.high[yp], plane.link[yp]
        low_sum, high_sum = low * odd_sum[yp], high * odd_sum[yp]
        value = link + high_sum * high
        if not edge:
            value = even_sum[yp] + (link + low_sum * low) + previous_row(value)
        centre.append(value)
        along.append(link - low_sum * high)
    low_e, low_o = plane.low
    high_e, high_o = plane.high
    low_n, high_n = next_lane(low_e), next_lane(high_e)
    first, second = low_o * odd_before, high_o * odd_before
    before = (second * high_e, second * low_e, first * high_e)
    if not edge:
        before = (even_before + first * low_e + previous_row(before[0]),) + before[1:]
    first, second = low_o * odd_after, high_o * odd_after
    after = (second * high_n, first * high_n, second * low_n)
    if not edge:
        after = (even_after + first * low_n + previous_row(after[0]),) + after[1:]
    low, high = plane.y_same
    cross = low * centre[1]
    side = high * before[0] + low * after[0] - cross * high
    middle = (
        centre[0]
        + low * (cross - before[0] - before[0])
        + previous_lane(high * (high * centre[1] - after[0] - after[0]))
    )
    low, high = plane.y
    low_next, high_next = plane.y_next
    one = low * along[1] + before[1]
    two = high * along[1] + after[2]
    up = (
        along[0]
        + low_next * one
        + low * before[2]
        + previous_lane(high_next * two + high * after[1]),
        high_next * one + low * after[1],
        low_next * two + high * before[2],
    )
    return Group(centre=middle, side=side, up=up)


def z_weights(below, middle, above):
    before = below + middle
    after = middle + above
    scale = inverse(before + after)
    return after * scale, before * scale


def with_lanes(value, value_next):
    return (value, next_lane(value), value_next, next_lane(value_next))


def between(weights, inner, low_link, high_link):
    lo, lo_j, lo_i, lo_ij = weights.lo
    hi, hi_j, hi_i, hi_ij = weights.hi
    (lo_s, lo_sj), (hi_s, hi_sj) = weights.lo_same, weights.hi_same

    def term(first, second, low, high, own):
        return second * (low + first * own) + first * high

    same = (
        hi_s * (low_link.same[0] - lo_s * inner.centre) + lo_s * high_link.same[0],
        term(lo_s, hi_sj, low_link.same[1], high_link.same[1], inner.side),
        term(lo_sj, hi_s, low_link.same[2], high_link.same[2], inner.side),
    )
    up = (
        term(lo, hi_i, low_link.up[0], high_link.up[0], inner.up[0]),
        term(lo, hi_ij, low_link.up[1], high_link.up[1], inner.up[1]),
        term(lo_j, hi_i, low_link.up[2], high_link.up[2], inner.up[2]),
    )
    down = (
        term(lo_i, hi, low_link.down[0], high_link.down[0], inner.up[0]),
        term(lo_i, hi_j, low_link.down[1], high_link.down[1], inner.up[2]),
        term(lo_ij, hi, low_link.down[2], high_link.down[2], inner.up[1]),
    )
    return same, up, down


def level(own, below, above):
    centre, side = own.centre, own.side
    up = list(own.up)
    weights, inner, link = below
    hi, hi_j, hi_i, hi_ij = weights.hi
    hi_s, hi_sj = weights.hi_same
    centre = centre + hi_s * (hi_s * inner.centre - link.same[0] - link.same[0])
    side = side + hi_s * (hi_sj * inner.side + link.same[1]) + hi_sj * link.same[2]
    up[0] = up[0] + hi * (hi_i * inner.up[0] + link.up[0]) + hi_i * link.down[0]
    up[1] = up[1] + hi * (hi_ij * inner.up[1] + link.up[1]) + hi_ij * link.down[2]
    up[2] = up[2] + hi_j * (hi_i * inner.up[2] + link.up[2]) + hi_i * link.down[1]
    weights, inner, link = above
    lo, lo_j, lo_i, lo_ij = weights.lo
    lo_s, lo_sj = weights.lo_same
    centre = centre + lo_s * (lo_s * inner.centre - link.same[0] - link.same[0])
    side = side + lo_sj * (lo_s * inner.side + link.same[1]) + lo_s * link.same[2]
    up[0] = up[0] + lo_i * (lo * inner.up[0] + link.up[0]) + lo * link.down[0]
    up[1] = up[1] + lo_ij * (lo * inner.up[1] + link.up[1]) + lo * link.down[2]
    up[2] = up[2] + lo_i * (lo_j * inner.up[2] + link.up[2]) + lo_j * link.down[1]
    return centre, side, up


def own_part(load, beyond, store):
    last = row_index() == 7

    def next_row(value, packed, p):
        return jnp.where(last, packed[p : p + 1, :], pltpu.roll(value, 7, 0))

    y_beyond = y_weights(beyond)[:2]
    z_beyond = z_weights(pltpu.roll(beyond[0], 1, 0), beyond[0], pltpu.roll(beyond[0], 7, 0))
    planes = []
    for p in range(7):
        even, odd = ([load(p, xp, yp) for yp in (0, 1)] for xp in (0, 1))
        even_next = [next_row(even[yp], beyond[yp], p) for yp in (0, 1)]
        low, high, before, after = y_weights(even)
        planes.append(
            Group(
                before=before,
                after=after,
                y=(low, high),
                y_same=(low, high),
                y_next=(next_row(low, y_beyond[0], p), next_row(high, y_beyond[1], p)),
                **x_weights(even, odd, even_next),
            )
        )
    links = [z_link(planes[p], planes[p + 1], False) for p in range(6)]
    inner = [None] * 7
    for p in range(1, 6):
        inner[p] = within(planes[p], links[p - 1].faces, links[p].faces, False)
    weights = [None] * 7
    for p in (1, 3, 5):
        lo, hi = z_weights(*(planes[p + n].even[0] for n in (-1, 0, 1)))
        lo = with_lanes(lo, next_row(lo, z_beyond[0], p))
        hi = with_lanes(hi, next_row(hi, z_beyond[1], p))
        weights[p] = Group(lo=lo, hi=hi, lo_same=lo[:2], hi_same=hi[:2])
    for p in (1, 3, 5):
        same, up, down = between(weights[p], inner[p], links[p - 1], links[p])
        plane = (p - 1) // 2
        if plane < 2:
            low = functools.partial(store, -1)
            low(0, 0, plane, same[0])
            low(0, 1, plane, same[2])
            low(0, -1, plane, previous_lane(same[1]))
            low(1, 0, plane, down[0])
            low(1, 1, plane, down[2])
            low(1, -1, plane, previous_lane(down[1]))
            low(-1, 0, plane, previous_row(up[0]))
            low(-1, 1, plane, previous_row(up[2]))
            low(-1, -1, plane, previous_lane(previous_row(up[1])))
        if plane > 0:
            high = functools.partial(store, 1)
            high(0, 0, plane - 1, same[0])
            high(0, 1, plane - 1, same[1])
            high(0, -1, plane - 1, previous_lane(same[2]))
            high(1, 0, plane - 1, up[0])
            high(1, 1, plane - 1, up[1])
            high(1, -1, plane - 1, previous_lane(up[2]))
            high(-1, 0, plane - 1, previous_row(down[0]))
            high(-1, 1, plane - 1, previous_row(down[1]))
            high(-1, -1, plane - 1, previous_lane(previous_row(down[2])))
    for plane in (0, 1):
        p = 2 * plane + 2
        centre, side, up = level(
            inner[p],
            (weights[p - 1], inner[p - 1], links[p - 1]),
            (weights[p + 1], inner[p + 1], links[p]),
        )
        here = functools.partial(store, 0)
        here(0, 0, plane, -centre)
        here(0, 1, plane, side)
        here(0, -1, plane, previous_lane(side))
        here(1, 0, plane, up[0])
        here(-1, 0, plane, previous_row(up[0]))
        here(1, 1, plane, up[1])
        here(-1, -1, plane, previous_lane(previous_row(up[1])))
        here(1, -1, plane, previous_lane(up[2]))
        here(-1, 1, plane, previous_row(up[2]))


def edge_part(even, odd, even_next, merge):
    low_next, high_next = y_weights(even_next)[:2]
    y_next = (low_next, high_next)
    plane = Group(
        y=y_weights(even)[:2],
        y_same=y_next,
        y_next=y_next,
        **x_weights(even, odd, even_next),
    )
    link = z_link(plane, plane.moved(1), True)
    link_below = link.moved(-1)
    inner = within(plane, link_below.faces, link.faces, True)

    def around(value):
        return (pltpu.roll(value, 1, 0), value, pltpu.roll(value, 7, 0))

    own, following = z_weights(*around(even[0])), z_weights(*around(even_next[0]))
    lo, hi = (with_lanes(own[n], following[n]) for n in (0, 1))
    weights = Group(lo=lo, hi=hi, lo_same=lo[2:], hi_same=hi[2:])
    same, up, down = between(weights, inner, link_below, link)
    centre, side, inside = level(
        inner,
        (weights.moved(-1), inner.moved(-1), link_below),
        (weights.moved(1), inner.moved(1), link),
    )
    rows = (1, 3)
    merge(-1, 0, 0, same[0], rows)
    merge(-1, 0, 1, same[2], rows)
    merge(-1, 0, -1, previous_lane(same[1]), rows)
    merge(-1, -1, 0, up[0], rows)
    merge(-1, -1, 1, up[2], rows)
    merge(-1, -1, -1, previous_lane(up[1]), rows)
    rows = (3, 5)
    merge(1, 0, 0, same[0], rows)
    merge(1, 0, 1, same[1], rows)
    merge(1, 0, -1, previous_lane(same[2]), rows)
    merge(1, -1, 0, down[0], rows)
    merge(1, -1, 1, down[1], rows)
    merge(1, -1, -1, previous_lane(down[2]), rows)
    rows = (2, 4)
    merge(0, 0, 0, -centre, rows)
    merge(0, 0, 1, side, rows)
    merge(0, 0, -1, previous_lane(side), rows)
    merge(0, -1, 0, inside[0], rows)
    merge(0, -1, -1, previous_lane(inside[1]), rows)
    merge(0, -1, 1, inside[2], rows)


def split_lanes(value):
    lane = lax.broadcasted_iota(jnp.int32, (value.shape[0], 128), 1)
    left, right = value[:, :128], value[:, 128:]
    first = (lane * 2) % 128 + lane // 64
    left = jnp.take_along_axis(left, first, axis=1)
    right = jnp.take_along_axis(right, (first + 1) % 2 + first // 2 * 2, axis=1)
    even = jnp.where(lane < 64, left, right)
    odd = pltpu.roll(jnp.where(lane < 64, right, left), 64, 1)
    return even, odd


SENT = {-1: (0, 1), 0: (0, 4), 1: (2, 2)}
LANDED = {-1: 6, 0: 2, 1: 0}
AHEAD = [(-1, 1), (1, 1), (0, 1)]
SIDE = [(-1, 0), (1, 0)]
BACK = [(0, -1), (-1, -1), (1, -1)]
MESSAGES = AHEAD + SIDE + BACK


def exchange_kernel(
    material,
    diffusivity,
    variation,
    out,
    blocks,
    facts,
    levels,
    borders,
    edges,
    split,
    tiles,
    beyond,
    load_sem,
    send_sem,
    recv_sem,
    here,
):
    gz, xy = lax.axis_index("gz"), lax.axis_index("xy")
    count_z, count_x = lax.axis_size("gz"), lax.axis_size("xy")
    inputs = (material, variation)

    def exists(dz, dx):
        inside = None
        for at, step, count in ((gz, dz, count_z), (xy, dx, count_x)):
            if step:
                good = at + step < count if step > 0 else at > 0
                inside = good if inside is None else jnp.logical_and(inside, good)
        return inside

    def device(dz, dx):
        return {"gz": gz + dz, "xy": xy + dx}

    def copies(dz, dx, origin=None):
        origin = inputs if origin is None else origin
        n = MESSAGES.index((dz, dx))
        first, planes = SENT[dz]
        made = []
        for which in (0, 1):
            source = origin[which].at[pl.ds(first, planes)]
            if dx == 0:
                target = borders[which].at[pl.ds(0 if dz > 0 else 2, planes)]
            else:
                row, rows, at = (14, 2, 6) if dx > 0 else (0, 1, 0)
                source = origin[which].at[pl.ds(first, planes), pl.ds(row, rows)]
                target = edges[0 if dx > 0 else 1][which].at[pl.ds(LANDED[dz], planes), pl.ds(at, rows)]
            made.append(
                pltpu.make_async_remote_copy(
                    src_ref=source,
                    dst_ref=target,
                    send_sem=send_sem.at[n, which],
                    recv_sem=recv_sem.at[n, which],
                    device_id=device(dz, dx),
                    device_id_type=MESH,
                )
            )
        return made

    def send(dz, dx, origin=None):
        @pl.when(exists(dz, dx))
        def _():
            for copy in copies(dz, dx, origin):
                copy.start()

    def receive(dz, dx):
        @pl.when(exists(-dz, -dx))
        def _():
            for copy in copies(dz, dx):
                copy.wait_recv()

    barrier = pltpu.get_barrier_semaphore()
    place_in_row = lax.rem(xy, ROW)
    first = jnp.logical_and(place_in_row == 0, xy > 0)
    last = jnp.logical_and(place_in_row == ROW - 1, xy < count_x - 1)
    inner = jnp.logical_not(jnp.logical_or(first, last))
    not_last = jnp.logical_not(last)
    before_last = lax.rem(xy + 1, ROW) == ROW - 1
    before_last = jnp.logical_and(before_last, xy < count_x - 2)

    def greet(semaphore, dz, dx, condition=None):
        good = exists(dz, dx)

        @pl.when(good if condition is None else jnp.logical_and(good, condition))
        def _():
            pl.semaphore_signal(
                semaphore, inc=1, device_id=device(dz, dx), device_id_type=MESH
            )

    loads = [
        pltpu.make_async_copy(source, target, load_sem.at[n])
        for n, (source, target) in enumerate(
            ((material, blocks), (variation, facts), (diffusivity, levels))
        )
    ]
    one = jnp.int32(1)
    z_sides = jnp.where(gz > 0, one, 0) + jnp.where(gz < count_z - 1, one, 0)

    @pl.when(last)
    def _():
        pl.semaphore_wait(barrier, z_sides + 1)
        for dz, dx in AHEAD:
            greet(here, dz, dx)
        for dz, dx in AHEAD:
            send(dz, dx)
        for dz, dx in BACK:
            greet(barrier, dz, dx)
        for copy in loads:
            copy.start()

    @pl.when(not_last)
    def _():
        for dz, dx in BACK + SIDE:
            greet(barrier, dz, dx)
        for dz, dx in AHEAD:
            greet(barrier, dz, dx, jnp.logical_not(before_last))
        for copy in loads:
            copy.start()
        expected = (
            z_sides
            + jnp.where(xy < count_x - 1, z_sides + 1, 0)
            + jnp.where(jnp.logical_and(inner, xy > 0), z_sides + 1, 0)
        )
        pl.semaphore_wait(barrier, expected)
        for dz, dx in AHEAD + SIDE:
            send(dz, dx)

    @pl.when(inner)
    def _():
        for dz, dx in BACK:
            send(dz, dx)

    def resistivity(which, factor):
        values = table
        for bit in (1, 2, 4):
            chosen = (which & bit) != 0
            values = [
                jnp.where(chosen, values[2 * n + 1], values[2 * n])
                for n in range(len(values) // 2)
            ]
        return -0.5 / (values[0] * factor)

    def place(plane, which, factor):
        for yp, half in enumerate(split_lanes(resistivity(which, factor))):
            split[plane, yp] = half
            for xp in (0, 1):
                rows = split[plane, yp, pl.ds(xp, 8, stride=2), :]
                tiles[xp, yp, pl.ds(8 * plane, 8), :] = rows

    for copy in loads:
        copy.wait()
    table = [levels[which] for which in range(8)]
    for k in range(4):
        place(k + 2, blocks[k], facts[k])

    @pl.when(last)
    def _():
        for dz, dx in AHEAD:
            receive(dz, dx)
        for dz, dx in BACK:
            send(dz, dx)
        for dz, dx in SIDE:
            send(dz, dx)

    for dz, dx in SIDE:
        receive(dz, dx)
    for n, plane in enumerate((0, 1, 6)):
        place(plane, borders[0][n], borders[1][n])
    for dz, dx in BACK:
        receive(dz, dx)

    @pl.when(gz == 0)
    def _():
        tiles[:, :, pl.ds(0, 16), :] = jnp.full((2, 2, 16, 128), OUTSIDE, jnp.float32)

    @pl.when(gz == count_z - 1)
    def _():
        tiles[:, :, pl.ds(48, 8), :] = jnp.full((2, 2, 8, 128), OUTSIDE, jnp.float32)

    outside = jnp.logical_or(
        jnp.logical_and(gz == 0, row_index() < 2),
        jnp.logical_and(gz == count_z - 1, row_index() == 6),
    )

    def spread(side):
        for plane in range(7):
            which, factor = (kind[plane] for kind in edges[side])
            for yp, half in enumerate(split_lanes(resistivity(which, factor))):
                beyond[side, yp, pl.ds(8 * plane, 8), :] = half

    def packed(side, row, missing):
        missing = jnp.logical_or(outside, missing)
        return [
            jnp.where(missing, OUTSIDE, beyond[side, yp, pl.ds(row, 8, stride=8), :])
            for yp in (0, 1)
        ]

    def entry(dz, dx, dy):
        return 9 * (dz + 1) + 3 * (dx + 1) + dy + 1

    def load(p, xp, yp):
        return tiles[xp, yp, pl.ds(8 * p, 8), :]

    def store(dz, dx, dy, plane, value):
        out[entry(dz, dx, dy), plane] = value

    spread(1)
    own_part(load, packed(1, 0, xy == count_x - 1), store)

    @pl.when(xy == count_x - 1)
    def _():
        for dz in (-1, 0, 1):
            for dy in (-1, 0, 1):
                for plane in (0, 1):
                    nothing = jnp.zeros((1, 128), jnp.float32)
                    out[entry(dz, 1, dy), plane, pl.ds(7, 1), :] = nothing

    @pl.when(first)
    def _():
        pl.semaphore_wait(here, z_sides + 1)
        for dz, dx in BACK:
            send(dz, dx, (blocks, facts))

    @pl.when(not_last)
    def _():
        for dz, dx in AHEAD:
            receive(dz, dx)

    spread(0)
    even_next = [tiles[0, yp, pl.ds(0, 8, stride=8), :] for yp in (0, 1)]

    def merge(dz, dx, dy, value, rows):
        if dx:
            value = jnp.where(xy > 0, value, 0.0)
        for plane, row in enumerate(rows):
            at = (entry(dz, dx, dy), plane, pl.ds(0, 1), slice(None))
            piece = value[row : row + 1, :]
            out[at] = piece if dx else out[at] + piece

    edge_part(packed(0, 6, xy == 0), packed(0, 7, xy == 0), even_next, merge)

    @pl.when(gz == 0)
    def _():
        out[0:9, 0] = jnp.zeros((9, 8, 128), jnp.float32)

    @pl.when(gz == count_z - 1)
    def _():
        out[18:27, 1] = jnp.zeros((9, 8, 128), jnp.float32)

    for dz, dx in MESSAGES:
        @pl.when(exists(dz, dx))
        def _():
            for copy in copies(dz, dx):
                copy.wait_send()


def write_kernel(result, out, sem):
    copy = pltpu.make_async_copy(result, out, sem.at[0])
    copy.start()
    copy.wait()


def per_device(material, diffusivity, variation):
    vmem = pl.BlockSpec(memory_space=pltpu.VMEM)
    material, diffusivity, variation = (
        pltpu.with_memory_space_constraint(x, pltpu.HBM)
        for x in (material, diffusivity, variation)
    )
    result = pl.pallas_call(
        exchange_kernel,
        out_shape=jax.ShapeDtypeStruct((27, 2, 8, 128), jnp.float32),
        in_specs=[
            pl.BlockSpec(memory_space=pltpu.HBM),
            pl.BlockSpec(memory_space=pltpu.HBM),
            pl.BlockSpec(memory_space=pltpu.HBM),
        ],
        out_specs=vmem,
        scratch_shapes=[
            pltpu.VMEM((4, 16, 256), jnp.int32),
            pltpu.VMEM((4, 16, 256), jnp.float32),
            pltpu.SMEM((8,), jnp.float32),
            [pltpu.VMEM((3, 16, 256), kind) for kind in (jnp.int32, jnp.float32)],
            [
                [pltpu.VMEM((7, 8, 256), kind) for kind in (jnp.int32, jnp.float32)]
                for _ in range(2)
            ],
            pltpu.VMEM((7, 2, 16, 128), jnp.float32),
            pltpu.VMEM((2, 2, 64, 128), jnp.float32),
            pltpu.VMEM((2, 2, 64, 128), jnp.float32),
            pltpu.SemaphoreType.DMA((3,)),
            pltpu.SemaphoreType.DMA((len(MESSAGES), 2)),
            pltpu.SemaphoreType.DMA((len(MESSAGES), 2)),
            pltpu.SemaphoreType.REGULAR,
        ],
        compiler_params=pltpu.CompilerParams(
            collective_id=0, has_side_effects=True, vmem_limit_bytes=VMEM_BYTES
        ),
        name="exchange",
    )(material, diffusivity, variation)
    return pl.pallas_call(
        write_kernel,
        out_shape=jax.ShapeDtypeStruct((27, 2, 8, 128), jnp.float32),
        in_specs=[vmem],
        out_specs=pl.BlockSpec(memory_space=pltpu.HBM),
        scratch_shapes=[pltpu.SemaphoreType.DMA((1,))],
        compiler_params=pltpu.CompilerParams(vmem_limit_bytes=VMEM_BYTES),
        name="write",
    )(result)


def solution(mesh):
    placed = (P("gz", "xy", None), P(), P("gz", "xy", None))
    return jax.shard_map(
        per_device, mesh=mesh, in_specs=placed, out_specs=P(None, "gz", "xy", None), check_vma=False
    )
```

```python
import functools

import jax
import jax.numpy as jnp
from jax import lax
from jax.experimental import pallas as pl
from jax.experimental.pallas import tpu as pltpu
from jax.sharding import PartitionSpec as P

MESH = pl.DeviceIdType.MESH
OUTSIDE = -1e-18
ROW = 16
VMEM_BYTES = 4 << 20


def row_index():
    return lax.broadcasted_iota(jnp.int32, (8, 128), 0)


def lane_index():
    return lax.broadcasted_iota(jnp.int32, (8, 128), 1)


def previous_row(value):
    return jnp.where(row_index() == 0, 0.0, pltpu.roll(value, 1, 0))


def next_lane(value):
    return pltpu.roll(value, 127, 1)


def previous_lane(value):
    return pltpu.roll(value, 1, 1)


def next_lane_bounded(value):
    return jnp.where(lane_index() == 127, OUTSIDE, next_lane(value))


def without_last(value):
    return jnp.where(lane_index() == 127, 0.0, value)


def inverse(value):
    return 1.0 / value


class Group:
    def __init__(self, **arrays):
        self.__dict__.update(arrays)

    def moved(self, step):
        def roll(value):
            if isinstance(value, (tuple, list)):
                return tuple(roll(part) for part in value)
            return value if value is None else pltpu.roll(value, -step % 8, 0)

        return Group(**{name: roll(value) for name, value in self.__dict__.items()})


def x_weights(even, odd, even_next):
    low, high, link = [], [], []
    for yp in (0, 1):
        before = even[yp] + odd[yp]
        after = odd[yp] + even_next[yp]
        scale = inverse(before + after)
        low.append(after * scale)
        high.append(before * scale)
        link.append(scale)
    return {"low": low, "high": high, "link": link, "odd": odd, "even": even}


def y_weights(even):
    before = even[0] + even[1]
    after = even[1] + next_lane_bounded(even[0])
    scale = inverse(before + after)
    return after * scale, without_last(before * scale), before, after


def z_link(lower, upper, edge):
    steps = []
    faces = []
    for yp in (0, 1):
        odd = inverse(lower.odd[yp] + upper.odd[yp])
        low, high = lower.low[yp] * odd, lower.high[yp] * odd
        same = high * upper.high[yp]
        even = None
        if not edge:
            even = inverse(lower.even[yp] + upper.even[yp])
            same = even + low * upper.low[yp] + previous_row(same)
        steps.append((same, low * upper.high[yp], high * upper.low[yp]))
        faces.append((even, odd))
    (even_same, even_up, even_down), (odd_same, odd_up, odd_down) = steps

    def y_step(even, odd, lower_y, upper_y):
        first, second = lower_y[0] * odd, lower_y[1] * odd
        return (
            even + first * upper_y[0] + previous_lane(second * upper_y[1]),
            first * upper_y[1],
            second * upper_y[0],
        )

    return Group(
        faces=tuple(faces),
        same=y_step(even_same, odd_same, lower.y_same, upper.y_same),
        up=y_step(even_up, odd_up, lower.y, upper.y_next),
        down=y_step(even_down, odd_down, lower.y_next, upper.y),
    )


def within(plane, faces_below, faces_above, edge):
    odd_e, odd_o = plane.odd

    def lower_face(face, rho):
        return jnp.where(lane_index() == 0, inverse(rho + OUTSIDE), previous_lane(face))

    odd_before = inverse(odd_e + odd_o)
    odd_after = inverse(odd_o + next_lane_bounded(odd_e))
    odd_sum = [
        odd_before + lower_face(odd_after, odd_e) + faces_below[0][1] + faces_above[0][1],
        odd_before + odd_after + faces_below[1][1] + faces_above[1][1],
    ]
    odd_after = without_last(odd_after)
    if not edge:
        even_before, even_after = inverse(plane.before), inverse(plane.after)
        even_lower = lower_face(even_after, plane.even[0])
        even_sum = [
            even_before + even_lower + faces_below[0][0] + faces_above[0][0],
            even_before + even_after + faces_below[1][0] + faces_above[1][0],
        ]
        even_after = without_last(even_after)
    centre, along = [], []
    for yp in (0, 1):
        low, high, link = plane.low[yp], plane.high[yp], plane.link[yp]
        low_sum, high_sum = low * odd_sum[yp], high * odd_sum[yp]
        value = link + high_sum * high
        if not edge:
            value = even_sum[yp] + (link + low_sum * low) + previous_row(value)
        centre.append(value)
        along.append(link - low_sum * high)
    low_e, low_o = plane.low
    high_e, high_o = plane.high
    low_n, high_n = next_lane(low_e), next_lane(high_e)
    first, second = low_o * odd_before, high_o * odd_before
    before = (second * high_e, second * low_e, first * high_e)
    if not edge:
        before = (even_before + first * low_e + previous_row(before[0]),) + before[1:]
    first, second = low_o * odd_after, high_o * odd_after
    after = (second * high_n, first * high_n, second * low_n)
    if not edge:
        after = (even_after + first * low_n + previous_row(after[0]),) + after[1:]
    low, high = plane.y_same
    cross = low * centre[1]
    side = high * before[0] + low * after[0] - cross * high
    middle = (
        centre[0]
        + low * (cross - before[0] - before[0])
        + previous_lane(high * (high * centre[1] - after[0] - after[0]))
    )
    low, high = plane.y
    low_next, high_next = plane.y_next
    one = low * along[1] + before[1]
    two = high * along[1] + after[2]
    up = (
        along[0]
        + low_next * one
        + low * before[2]
        + previous_lane(high_next * two + high * after[1]),
        high_next * one + low * after[1],
        low_next * two + high * before[2],
    )
    return Group(centre=middle, side=side, up=up)


def z_weights(below, middle, above):
    before = below + middle
    after = middle + above
    scale = inverse(before + after)
    return after * scale, before * scale


def with_lanes(value, value_next):
    return (value, next_lane(value), value_next, next_lane(value_next))


def between(weights, inner, low_link, high_link):
    lo, lo_j, lo_i, lo_ij = weights.lo
    hi, hi_j, hi_i, hi_ij = weights.hi
    (lo_s, lo_sj), (hi_s, hi_sj) = weights.lo_same, weights.hi_same

    def term(first, second, low, high, own):
        return second * (low + first * own) + first * high

    same = (
        hi_s * (low_link.same[0] - lo_s * inner.centre) + lo_s * high_link.same[0],
        term(lo_s, hi_sj, low_link.same[1], high_link.same[1], inner.side),
        term(lo_sj, hi_s, low_link.same[2], high_link.same[2], inner.side),
    )
    up = (
        term(lo, hi_i, low_link.up[0], high_link.up[0], inner.up[0]),
        term(lo, hi_ij, low_link.up[1], high_link.up[1], inner.up[1]),
        term(lo_j, hi_i, low_link.up[2], high_link.up[2], inner.up[2]),
    )
    down = (
        term(lo_i, hi, low_link.down[0], high_link.down[0], inner.up[0]),
        term(lo_i, hi_j, low_link.down[1], high_link.down[1], inner.up[2]),
        term(lo_ij, hi, low_link.down[2], high_link.down[2], inner.up[1]),
    )
    return same, up, down


def level(own, below, above):
    centre, side = own.centre, own.side
    up = list(own.up)
    weights, inner, link = below
    hi, hi_j, hi_i, hi_ij = weights.hi
    hi_s, hi_sj = weights.hi_same
    centre = centre + hi_s * (hi_s * inner.centre - link.same[0] - link.same[0])
    side = side + hi_s * (hi_sj * inner.side + link.same[1]) + hi_sj * link.same[2]
    up[0] = up[0] + hi * (hi_i * inner.up[0] + link.up[0]) + hi_i * link.down[0]
    up[1] = up[1] + hi * (hi_ij * inner.up[1] + link.up[1]) + hi_ij * link.down[2]
    up[2] = up[2] + hi_j * (hi_i * inner.up[2] + link.up[2]) + hi_i * link.down[1]
    weights, inner, link = above
    lo, lo_j, lo_i, lo_ij = weights.lo
    lo_s, lo_sj = weights.lo_same
    centre = centre + lo_s * (lo_s * inner.centre - link.same[0] - link.same[0])
    side = side + lo_sj * (lo_s * inner.side + link.same[1]) + lo_s * link.same[2]
    up[0] = up[0] + lo_i * (lo * inner.up[0] + link.up[0]) + lo * link.down[0]
    up[1] = up[1] + lo_ij * (lo * inner.up[1] + link.up[1]) + lo * link.down[2]
    up[2] = up[2] + lo_i * (lo_j * inner.up[2] + link.up[2]) + lo_j * link.down[1]
    return centre, side, up


def own_part(load, beyond, store):
    last = row_index() == 7

    def next_row(value, packed, p):
        return jnp.where(last, packed[p : p + 1, :], pltpu.roll(value, 7, 0))

    y_beyond = y_weights(beyond)[:2]
    z_beyond = z_weights(pltpu.roll(beyond[0], 1, 0), beyond[0], pltpu.roll(beyond[0], 7, 0))
    planes = []
    for p in range(7):
        even, odd = ([load(p, xp, yp) for yp in (0, 1)] for xp in (0, 1))
        even_next = [next_row(even[yp], beyond[yp], p) for yp in (0, 1)]
        low, high, before, after = y_weights(even)
        planes.append(
            Group(
                before=before,
                after=after,
                y=(low, high),
                y_same=(low, high),
                y_next=(next_row(low, y_beyond[0], p), next_row(high, y_beyond[1], p)),
                **x_weights(even, odd, even_next),
            )
        )
    links = [z_link(planes[p], planes[p + 1], False) for p in range(6)]
    inner = [None] * 7
    for p in range(1, 6):
        inner[p] = within(planes[p], links[p - 1].faces, links[p].faces, False)
    weights = [None] * 7
    for p in (1, 3, 5):
        lo, hi = z_weights(*(planes[p + n].even[0] for n in (-1, 0, 1)))
        lo = with_lanes(lo, next_row(lo, z_beyond[0], p))
        hi = with_lanes(hi, next_row(hi, z_beyond[1], p))
        weights[p] = Group(lo=lo, hi=hi, lo_same=lo[:2], hi_same=hi[:2])
    for p in (1, 3, 5):
        same, up, down = between(weights[p], inner[p], links[p - 1], links[p])
        plane = (p - 1) // 2
        if plane < 2:
            low = functools.partial(store, -1)
            low(0, 0, plane, same[0])
            low(0, 1, plane, same[2])
            low(0, -1, plane, previous_lane(same[1]))
            low(1, 0, plane, down[0])
            low(1, 1, plane, down[2])
            low(1, -1, plane, previous_lane(down[1]))
            low(-1, 0, plane, previous_row(up[0]))
            low(-1, 1, plane, previous_row(up[2]))
            low(-1, -1, plane, previous_lane(previous_row(up[1])))
        if plane > 0:
            high = functools.partial(store, 1)
            high(0, 0, plane - 1, same[0])
            high(0, 1, plane - 1, same[1])
            high(0, -1, plane - 1, previous_lane(same[2]))
            high(1, 0, plane - 1, up[0])
            high(1, 1, plane - 1, up[1])
            high(1, -1, plane - 1, previous_lane(up[2]))
            high(-1, 0, plane - 1, previous_row(down[0]))
            high(-1, 1, plane - 1, previous_row(down[1]))
            high(-1, -1, plane - 1, previous_lane(previous_row(down[2])))
    for plane in (0, 1):
        p = 2 * plane + 2
        centre, side, up = level(
            inner[p],
            (weights[p - 1], inner[p - 1], links[p - 1]),
            (weights[p + 1], inner[p + 1], links[p]),
        )
        here = functools.partial(store, 0)
        here(0, 0, plane, -centre)
        here(0, 1, plane, side)
        here(0, -1, plane, previous_lane(side))
        here(1, 0, plane, up[0])
        here(-1, 0, plane, previous_row(up[0]))
        here(1, 1, plane, up[1])
        here(-1, -1, plane, previous_lane(previous_row(up[1])))
        here(1, -1, plane, previous_lane(up[2]))
        here(-1, 1, plane, previous_row(up[2]))


def edge_part(even, odd, even_next, merge):
    low_next, high_next = y_weights(even_next)[:2]
    y_next = (low_next, high_next)
    plane = Group(
        y=y_weights(even)[:2],
        y_same=y_next,
        y_next=y_next,
        **x_weights(even, odd, even_next),
    )
    link = z_link(plane, plane.moved(1), True)
    link_below = link.moved(-1)
    inner = within(plane, link_below.faces, link.faces, True)

    def around(value):
        return (pltpu.roll(value, 1, 0), value, pltpu.roll(value, 7, 0))

    own, following = z_weights(*around(even[0])), z_weights(*around(even_next[0]))
    lo, hi = (with_lanes(own[n], following[n]) for n in (0, 1))
    weights = Group(lo=lo, hi=hi, lo_same=lo[2:], hi_same=hi[2:])
    same, up, down = between(weights, inner, link_below, link)
    centre, side, inside = level(
        inner,
        (weights.moved(-1), inner.moved(-1), link_below),
        (weights.moved(1), inner.moved(1), link),
    )
    rows = (1, 3)
    merge(-1, 0, 0, same[0], rows)
    merge(-1, 0, 1, same[2], rows)
    merge(-1, 0, -1, previous_lane(same[1]), rows)
    merge(-1, -1, 0, up[0], rows)
    merge(-1, -1, 1, up[2], rows)
    merge(-1, -1, -1, previous_lane(up[1]), rows)
    rows = (3, 5)
    merge(1, 0, 0, same[0], rows)
    merge(1, 0, 1, same[1], rows)
    merge(1, 0, -1, previous_lane(same[2]), rows)
    merge(1, -1, 0, down[0], rows)
    merge(1, -1, 1, down[1], rows)
    merge(1, -1, -1, previous_lane(down[2]), rows)
    rows = (2, 4)
    merge(0, 0, 0, -centre, rows)
    merge(0, 0, 1, side, rows)
    merge(0, 0, -1, previous_lane(side), rows)
    merge(0, -1, 0, inside[0], rows)
    merge(0, -1, -1, previous_lane(inside[1]), rows)
    merge(0, -1, 1, inside[2], rows)


def split_lanes(value):
    lane = lax.broadcasted_iota(jnp.int32, (value.shape[0], 128), 1)
    left, right = value[:, :128], value[:, 128:]
    first = (lane * 2) % 128 + lane // 64
    left = jnp.take_along_axis(left, first, axis=1)
    right = jnp.take_along_axis(right, (first + 1) % 2 + first // 2 * 2, axis=1)
    even = jnp.where(lane < 64, left, right)
    odd = pltpu.roll(jnp.where(lane < 64, right, left), 64, 1)
    return even, odd


SENT = {-1: (0, 1), 0: (0, 4), 1: (2, 2)}
LANDED = {-1: 6, 0: 2, 1: 0}
AHEAD = [(-1, 1), (0, 1), (1, 1)]
SIDE = [(-1, 0), (1, 0)]
BACK = [(0, -1), (-1, -1), (1, -1)]
MESSAGES = AHEAD + SIDE + BACK


def exchange_kernel(
    material,
    diffusivity,
    variation,
    out,
    blocks,
    facts,
    levels,
    borders,
    edges,
    split,
    tiles,
    beyond,
    load_sem,
    send_sem,
    recv_sem,
    here,
):
    gz, xy = lax.axis_index("gz"), lax.axis_index("xy")
    count_z, count_x = lax.axis_size("gz"), lax.axis_size("xy")
    inputs = (material, variation)

    def exists(dz, dx):
        inside = None
        for at, step, count in ((gz, dz, count_z), (xy, dx, count_x)):
            if step:
                good = at + step < count if step > 0 else at > 0
                inside = good if inside is None else jnp.logical_and(inside, good)
        return inside

    def device(dz, dx):
        return {"gz": gz + dz, "xy": xy + dx}

    def copies(dz, dx, origin=None):
        origin = inputs if origin is None else origin
        n = MESSAGES.index((dz, dx))
        first, planes = SENT[dz]
        made = []
        for which in (0, 1):
            source = origin[which].at[pl.ds(first, planes)]
            if dx == 0:
                target = borders[which].at[pl.ds(0 if dz > 0 else 2, planes)]
            else:
                row, rows, at = (14, 2, 6) if dx > 0 else (0, 1, 0)
                source = origin[which].at[pl.ds(first, planes), pl.ds(row, rows)]
                target = edges[0 if dx > 0 else 1][which].at[pl.ds(LANDED[dz], planes), pl.ds(at, rows)]
            made.append(
                pltpu.make_async_remote_copy(
                    src_ref=source,
                    dst_ref=target,
                    send_sem=send_sem.at[n, which],
                    recv_sem=recv_sem.at[n, which],
                    device_id=device(dz, dx),
                    device_id_type=MESH,
                )
            )
        return made

    def send(dz, dx, origin=None):
        @pl.when(exists(dz, dx))
        def _():
            for copy in copies(dz, dx, origin):
                copy.start()

    def receive(dz, dx):
        @pl.when(exists(-dz, -dx))
        def _():
            for copy in copies(dz, dx):
                copy.wait_recv()

    barrier = pltpu.get_barrier_semaphore()
    place_in_row = lax.rem(xy, ROW)
    first = jnp.logical_and(place_in_row == 0, xy > 0)
    last = jnp.logical_and(place_in_row == ROW - 1, xy < count_x - 1)
    inner = jnp.logical_not(jnp.logical_or(first, last))
    not_last = jnp.logical_not(last)
    before_last = lax.rem(xy + 1, ROW) == ROW - 1
    before_last = jnp.logical_and(before_last, xy < count_x - 2)

    def greet(semaphore, dz, dx, condition=None):
        good = exists(dz, dx)

        @pl.when(good if condition is None else jnp.logical_and(good, condition))
        def _():
            pl.semaphore_signal(
                semaphore, inc=1, device_id=device(dz, dx), device_id_type=MESH
            )

    loads = [
        pltpu.make_async_copy(source, target, load_sem.at[n])
        for n, (source, target) in enumerate(
            ((material, blocks), (variation, facts), (diffusivity, levels))
        )
    ]
    one = jnp.int32(1)
    z_sides = jnp.where(gz > 0, one, 0) + jnp.where(gz < count_z - 1, one, 0)

    @pl.when(last)
    def _():
        pl.semaphore_wait(barrier, z_sides + 1)
        send(*AHEAD[0])
        for dz, dx in AHEAD:
            greet(here, dz, dx)
        for dz, dx in AHEAD[1:]:
            send(dz, dx)
        for dz, dx in BACK:
            greet(barrier, dz, dx)
        for copy in loads:
            copy.start()

    @pl.when(not_last)
    def _():
        for dz, dx in BACK + SIDE:
            greet(barrier, dz, dx)
        for dz, dx in AHEAD:
            greet(barrier, dz, dx, jnp.logical_not(before_last))
        for copy in loads:
            copy.start()
        expected = (
            z_sides
            + jnp.where(xy < count_x - 1, z_sides + 1, 0)
            + jnp.where(jnp.logical_and(inner, xy > 0), z_sides + 1, 0)
        )
        pl.semaphore_wait(barrier, expected)
        for dz, dx in AHEAD + SIDE:
            send(dz, dx)

    @pl.when(inner)
    def _():
        for dz, dx in BACK:
            send(dz, dx)

    def resistivity(which, factor):
        values = table
        for bit in (1, 2, 4):
            chosen = (which & bit) != 0
            values = [
                jnp.where(chosen, values[2 * n + 1], values[2 * n])
                for n in range(len(values) // 2)
            ]
        return -0.5 / (values[0] * factor)

    def place(plane, which, factor):
        for yp, half in enumerate(split_lanes(resistivity(which, factor))):
            split[plane, yp] = half
            for xp in (0, 1):
                rows = split[plane, yp, pl.ds(xp, 8, stride=2), :]
                tiles[xp, yp, pl.ds(8 * plane, 8), :] = rows

    for copy in loads:
        copy.wait()
    table = [levels[which] for which in range(8)]
    for k in range(4):
        place(k + 2, blocks[k], facts[k])

    @pl.when(last)
    def _():
        for dz, dx in AHEAD:
            receive(dz, dx)
        for dz, dx in BACK:
            send(dz, dx)
        for dz, dx in SIDE:
            send(dz, dx)

    for dz, dx in SIDE:
        receive(dz, dx)
    for n, plane in enumerate((0, 1, 6)):
        place(plane, borders[0][n], borders[1][n])
    for dz, dx in BACK:
        receive(dz, dx)

    @pl.when(gz == 0)
    def _():
        tiles[:, :, pl.ds(0, 16), :] = jnp.full((2, 2, 16, 128), OUTSIDE, jnp.float32)

    @pl.when(gz == count_z - 1)
    def _():
        tiles[:, :, pl.ds(48, 8), :] = jnp.full((2, 2, 8, 128), OUTSIDE, jnp.float32)

    outside = jnp.logical_or(
        jnp.logical_and(gz == 0, row_index() < 2),
        jnp.logical_and(gz == count_z - 1, row_index() == 6),
    )

    def spread(side, some):
        for plane in some:
            which, factor = (kind[plane] for kind in edges[side])
            for yp, half in enumerate(split_lanes(resistivity(which, factor))):
                beyond[side, yp, pl.ds(8 * plane, 8), :] = half

    def packed(side, row, missing):
        missing = jnp.logical_or(outside, missing)
        return [
            jnp.where(missing, OUTSIDE, beyond[side, yp, pl.ds(row, 8, stride=8), :])
            for yp in (0, 1)
        ]

    def entry(dz, dx, dy):
        return 9 * (dz + 1) + 3 * (dx + 1) + dy + 1

    def load(p, xp, yp):
        return tiles[xp, yp, pl.ds(8 * p, 8), :]

    def store(dz, dx, dy, plane, value):
        out[entry(dz, dx, dy), plane] = value

    spread(1, range(7))
    own_part(load, packed(1, 0, xy == count_x - 1), store)

    @pl.when(xy == count_x - 1)
    def _():
        for dz in (-1, 0, 1):
            for dy in (-1, 0, 1):
                for plane in (0, 1):
                    nothing = jnp.zeros((1, 128), jnp.float32)
                    out[entry(dz, 1, dy), plane, pl.ds(7, 1), :] = nothing

    @pl.when(first)
    def _():
        pl.semaphore_wait(here, z_sides + 1)
        for dz, dx in BACK:
            send(dz, dx, (blocks, facts))

    for dz, dx in ((0, 1), (1, 1), (-1, 1)):

        @pl.when(not_last)
        def _():
            receive(dz, dx)

        spread(0, range(LANDED[dz], LANDED[dz] + SENT[dz][1]))
    even_next = [tiles[0, yp, pl.ds(0, 8, stride=8), :] for yp in (0, 1)]

    def merge(dz, dx, dy, value, rows):
        if dx:
            value = jnp.where(xy > 0, value, 0.0)
        for plane, row in enumerate(rows):
            at = (entry(dz, dx, dy), plane, pl.ds(0, 1), slice(None))
            piece = value[row : row + 1, :]
            out[at] = piece if dx else out[at] + piece

    edge_part(packed(0, 6, xy == 0), packed(0, 7, xy == 0), even_next, merge)

    @pl.when(gz == 0)
    def _():
        out[0:9, 0] = jnp.zeros((9, 8, 128), jnp.float32)

    @pl.when(gz == count_z - 1)
    def _():
        out[18:27, 1] = jnp.zeros((9, 8, 128), jnp.float32)

    for dz, dx in MESSAGES:
        @pl.when(exists(dz, dx))
        def _():
            for copy in copies(dz, dx):
                copy.wait_send()


def write_kernel(result, out, sem):
    copy = pltpu.make_async_copy(result, out, sem.at[0])
    copy.start()
    copy.wait()


def per_device(material, diffusivity, variation):
    vmem = pl.BlockSpec(memory_space=pltpu.VMEM)
    material, diffusivity, variation = (
        pltpu.with_memory_space_constraint(x, pltpu.HBM)
        for x in (material, diffusivity, variation)
    )
    result = pl.pallas_call(
        exchange_kernel,
        out_shape=jax.ShapeDtypeStruct((27, 2, 8, 128), jnp.float32),
        in_specs=[
            pl.BlockSpec(memory_space=pltpu.HBM),
            pl.BlockSpec(memory_space=pltpu.HBM),
            pl.BlockSpec(memory_space=pltpu.HBM),
        ],
        out_specs=vmem,
        scratch_shapes=[
            pltpu.VMEM((4, 16, 256), jnp.int32),
            pltpu.VMEM((4, 16, 256), jnp.float32),
            pltpu.SMEM((8,), jnp.float32),
            [pltpu.VMEM((3, 16, 256), kind) for kind in (jnp.int32, jnp.float32)],
            [
                [pltpu.VMEM((7, 8, 256), kind) for kind in (jnp.int32, jnp.float32)]
                for _ in range(2)
            ],
            pltpu.VMEM((7, 2, 16, 128), jnp.float32),
            pltpu.VMEM((2, 2, 64, 128), jnp.float32),
            pltpu.VMEM((2, 2, 64, 128), jnp.float32),
            pltpu.SemaphoreType.DMA((3,)),
            pltpu.SemaphoreType.DMA((len(MESSAGES), 2)),
            pltpu.SemaphoreType.DMA((len(MESSAGES), 2)),
            pltpu.SemaphoreType.REGULAR,
        ],
        compiler_params=pltpu.CompilerParams(
            collective_id=0, has_side_effects=True, vmem_limit_bytes=VMEM_BYTES
        ),
        name="exchange",
    )(material, diffusivity, variation)
    return pl.pallas_call(
        write_kernel,
        out_shape=jax.ShapeDtypeStruct((27, 2, 8, 128), jnp.float32),
        in_specs=[vmem],
        out_specs=pl.BlockSpec(memory_space=pltpu.HBM),
        scratch_shapes=[pltpu.SemaphoreType.DMA((1,))],
        compiler_params=pltpu.CompilerParams(vmem_limit_bytes=VMEM_BYTES),
        name="write",
    )(result)


def solution(mesh):
    placed = (P("gz", "xy", None), P(), P("gz", "xy", None))
    return jax.shard_map(
        per_device, mesh=mesh, in_specs=placed, out_specs=P(None, "gz", "xy", None), check_vma=False
    )
```

```python
import functools

import jax
import jax.numpy as jnp
from jax import lax
from jax.experimental import pallas as pl
from jax.experimental.pallas import tpu as pltpu
from jax.sharding import PartitionSpec as P

MESH = pl.DeviceIdType.MESH
OUTSIDE = -1e-18
ROW = 16
VMEM_BYTES = 4 << 20


def row_index():
    return lax.broadcasted_iota(jnp.int32, (8, 128), 0)


def lane_index():
    return lax.broadcasted_iota(jnp.int32, (8, 128), 1)


def previous_row(value):
    return jnp.where(row_index() == 0, 0.0, pltpu.roll(value, 1, 0))


def next_lane(value):
    return pltpu.roll(value, 127, 1)


def previous_lane(value):
    return pltpu.roll(value, 1, 1)


def next_lane_bounded(value):
    return jnp.where(lane_index() == 127, OUTSIDE, next_lane(value))


def without_last(value):
    return jnp.where(lane_index() == 127, 0.0, value)


def inverse(value):
    return 1.0 / value


class Group:
    def __init__(self, **arrays):
        self.__dict__.update(arrays)

    def moved(self, step):
        def roll(value):
            if isinstance(value, (tuple, list)):
                return tuple(roll(part) for part in value)
            return value if value is None else pltpu.roll(value, -step % 8, 0)

        return Group(**{name: roll(value) for name, value in self.__dict__.items()})


def x_weights(even, odd, even_next):
    low, high, link = [], [], []
    for yp in (0, 1):
        before = even[yp] + odd[yp]
        after = odd[yp] + even_next[yp]
        scale = inverse(before + after)
        low.append(after * scale)
        high.append(before * scale)
        link.append(scale)
    return {"low": low, "high": high, "link": link, "odd": odd, "even": even}


def y_weights(even):
    before = even[0] + even[1]
    after = even[1] + next_lane_bounded(even[0])
    scale = inverse(before + after)
    return after * scale, without_last(before * scale), before, after


def z_link(lower, upper, edge):
    steps = []
    faces = []
    for yp in (0, 1):
        odd = inverse(lower.odd[yp] + upper.odd[yp])
        low, high = lower.low[yp] * odd, lower.high[yp] * odd
        same = high * upper.high[yp]
        even = None
        if not edge:
            even = inverse(lower.even[yp] + upper.even[yp])
            same = even + low * upper.low[yp] + previous_row(same)
        steps.append((same, low * upper.high[yp], high * upper.low[yp]))
        faces.append((even, odd))
    (even_same, even_up, even_down), (odd_same, odd_up, odd_down) = steps

    def y_step(even, odd, lower_y, upper_y):
        first, second = lower_y[0] * odd, lower_y[1] * odd
        return (
            even + first * upper_y[0] + previous_lane(second * upper_y[1]),
            first * upper_y[1],
            second * upper_y[0],
        )

    return Group(
        faces=tuple(faces),
        same=y_step(even_same, odd_same, lower.y_same, upper.y_same),
        up=y_step(even_up, odd_up, lower.y, upper.y_next),
        down=y_step(even_down, odd_down, lower.y_next, upper.y),
    )


def within(plane, faces_below, faces_above, edge):
    odd_e, odd_o = plane.odd

    def lower_face(face, rho):
        return jnp.where(lane_index() == 0, inverse(rho + OUTSIDE), previous_lane(face))

    odd_before = inverse(odd_e + odd_o)
    odd_after = inverse(odd_o + next_lane_bounded(odd_e))
    odd_sum = [
        odd_before + lower_face(odd_after, odd_e) + faces_below[0][1] + faces_above[0][1],
        odd_before + odd_after + faces_below[1][1] + faces_above[1][1],
    ]
    odd_after = without_last(odd_after)
    if not edge:
        even_before, even_after = inverse(plane.before), inverse(plane.after)
        even_lower = lower_face(even_after, plane.even[0])
        even_sum = [
            even_before + even_lower + faces_below[0][0] + faces_above[0][0],
            even_before + even_after + faces_below[1][0] + faces_above[1][0],
        ]
        even_after = without_last(even_after)
    centre, along = [], []
    for yp in (0, 1):
        low, high, link = plane.low[yp], plane.high[yp], plane.link[yp]
        low_sum, high_sum = low * odd_sum[yp], high * odd_sum[yp]
        value = link + high_sum * high
        if not edge:
            value = even_sum[yp] + (link + low_sum * low) + previous_row(value)
        centre.append(value)
        along.append(link - low_sum * high)
    low_e, low_o = plane.low
    high_e, high_o = plane.high
    low_n, high_n = next_lane(low_e), next_lane(high_e)
    first, second = low_o * odd_before, high_o * odd_before
    before = (second * high_e, second * low_e, first * high_e)
    if not edge:
        before = (even_before + first * low_e + previous_row(before[0]),) + before[1:]
    first, second = low_o * odd_after, high_o * odd_after
    after = (second * high_n, first * high_n, second * low_n)
    if not edge:
        after = (even_after + first * low_n + previous_row(after[0]),) + after[1:]
    low, high = plane.y_same
    cross = low * centre[1]
    side = high * before[0] + low * after[0] - cross * high
    middle = (
        centre[0]
        + low * (cross - before[0] - before[0])
        + previous_lane(high * (high * centre[1] - after[0] - after[0]))
    )
    low, high = plane.y
    low_next, high_next = plane.y_next
    one = low * along[1] + before[1]
    two = high * along[1] + after[2]
    up = (
        along[0]
        + low_next * one
        + low * before[2]
        + previous_lane(high_next * two + high * after[1]),
        high_next * one + low * after[1],
        low_next * two + high * before[2],
    )
    return Group(centre=middle, side=side, up=up)


def z_weights(below, middle, above):
    before = below + middle
    after = middle + above
    scale = inverse(before + after)
    return after * scale, before * scale


def with_lanes(value, value_next):
    return (value, next_lane(value), value_next, next_lane(value_next))


def between(weights, inner, low_link, high_link):
    lo, lo_j, lo_i, lo_ij = weights.lo
    hi, hi_j, hi_i, hi_ij = weights.hi
    (lo_s, lo_sj), (hi_s, hi_sj) = weights.lo_same, weights.hi_same

    def term(first, second, low, high, own):
        return second * (low + first * own) + first * high

    same = (
        hi_s * (low_link.same[0] - lo_s * inner.centre) + lo_s * high_link.same[0],
        term(lo_s, hi_sj, low_link.same[1], high_link.same[1], inner.side),
        term(lo_sj, hi_s, low_link.same[2], high_link.same[2], inner.side),
    )
    up = (
        term(lo, hi_i, low_link.up[0], high_link.up[0], inner.up[0]),
        term(lo, hi_ij, low_link.up[1], high_link.up[1], inner.up[1]),
        term(lo_j, hi_i, low_link.up[2], high_link.up[2], inner.up[2]),
    )
    down = (
        term(lo_i, hi, low_link.down[0], high_link.down[0], inner.up[0]),
        term(lo_i, hi_j, low_link.down[1], high_link.down[1], inner.up[2]),
        term(lo_ij, hi, low_link.down[2], high_link.down[2], inner.up[1]),
    )
    return same, up, down


def level(own, below, above):
    centre, side = own.centre, own.side
    up = list(own.up)
    weights, inner, link = below
    hi, hi_j, hi_i, hi_ij = weights.hi
    hi_s, hi_sj = weights.hi_same
    centre = centre + hi_s * (hi_s * inner.centre - link.same[0] - link.same[0])
    side = side + hi_s * (hi_sj * inner.side + link.same[1]) + hi_sj * link.same[2]
    up[0] = up[0] + hi * (hi_i * inner.up[0] + link.up[0]) + hi_i * link.down[0]
    up[1] = up[1] + hi * (hi_ij * inner.up[1] + link.up[1]) + hi_ij * link.down[2]
    up[2] = up[2] + hi_j * (hi_i * inner.up[2] + link.up[2]) + hi_i * link.down[1]
    weights, inner, link = above
    lo, lo_j, lo_i, lo_ij = weights.lo
    lo_s, lo_sj = weights.lo_same
    centre = centre + lo_s * (lo_s * inner.centre - link.same[0] - link.same[0])
    side = side + lo_sj * (lo_s * inner.side + link.same[1]) + lo_s * link.same[2]
    up[0] = up[0] + lo_i * (lo * inner.up[0] + link.up[0]) + lo * link.down[0]
    up[1] = up[1] + lo_ij * (lo * inner.up[1] + link.up[1]) + lo * link.down[2]
    up[2] = up[2] + lo_i * (lo_j * inner.up[2] + link.up[2]) + lo_j * link.down[1]
    return centre, side, up


def own_part(load, beyond, store):
    last = row_index() == 7

    def next_row(value, packed, p):
        return jnp.where(last, packed[p : p + 1, :], pltpu.roll(value, 7, 0))

    y_beyond = y_weights(beyond)[:2]
    z_beyond = z_weights(pltpu.roll(beyond[0], 1, 0), beyond[0], pltpu.roll(beyond[0], 7, 0))
    planes = []
    for p in range(7):
        even, odd = ([load(p, xp, yp) for yp in (0, 1)] for xp in (0, 1))
        even_next = [next_row(even[yp], beyond[yp], p) for yp in (0, 1)]
        low, high, before, after = y_weights(even)
        planes.append(
            Group(
                before=before,
                after=after,
                y=(low, high),
                y_same=(low, high),
                y_next=(next_row(low, y_beyond[0], p), next_row(high, y_beyond[1], p)),
                **x_weights(even, odd, even_next),
            )
        )
    links = [z_link(planes[p], planes[p + 1], False) for p in range(6)]
    inner = [None] * 7
    for p in range(1, 6):
        inner[p] = within(planes[p], links[p - 1].faces, links[p].faces, False)
    weights = [None] * 7
    for p in (1, 3, 5):
        lo, hi = z_weights(*(planes[p + n].even[0] for n in (-1, 0, 1)))
        lo = with_lanes(lo, next_row(lo, z_beyond[0], p))
        hi = with_lanes(hi, next_row(hi, z_beyond[1], p))
        weights[p] = Group(lo=lo, hi=hi, lo_same=lo[:2], hi_same=hi[:2])
    for p in (1, 3, 5):
        same, up, down = between(weights[p], inner[p], links[p - 1], links[p])
        plane = (p - 1) // 2
        if plane < 2:
            low = functools.partial(store, -1)
            low(0, 0, plane, same[0])
            low(0, 1, plane, same[2])
            low(0, -1, plane, previous_lane(same[1]))
            low(1, 0, plane, down[0])
            low(1, 1, plane, down[2])
            low(1, -1, plane, previous_lane(down[1]))
            low(-1, 0, plane, previous_row(up[0]))
            low(-1, 1, plane, previous_row(up[2]))
            low(-1, -1, plane, previous_lane(previous_row(up[1])))
        if plane > 0:
            high = functools.partial(store, 1)
            high(0, 0, plane - 1, same[0])
            high(0, 1, plane - 1, same[1])
            high(0, -1, plane - 1, previous_lane(same[2]))
            high(1, 0, plane - 1, up[0])
            high(1, 1, plane - 1, up[1])
            high(1, -1, plane - 1, previous_lane(up[2]))
            high(-1, 0, plane - 1, previous_row(down[0]))
            high(-1, 1, plane - 1, previous_row(down[1]))
            high(-1, -1, plane - 1, previous_lane(previous_row(down[2])))
    for plane in (0, 1):
        p = 2 * plane + 2
        centre, side, up = level(
            inner[p],
            (weights[p - 1], inner[p - 1], links[p - 1]),
            (weights[p + 1], inner[p + 1], links[p]),
        )
        here = functools.partial(store, 0)
        here(0, 0, plane, -centre)
        here(0, 1, plane, side)
        here(0, -1, plane, previous_lane(side))
        here(1, 0, plane, up[0])
        here(-1, 0, plane, previous_row(up[0]))
        here(1, 1, plane, up[1])
        here(-1, -1, plane, previous_lane(previous_row(up[1])))
        here(1, -1, plane, previous_lane(up[2]))
        here(-1, 1, plane, previous_row(up[2]))


def edge_part(even, odd, even_next, merge):
    low_next, high_next = y_weights(even_next)[:2]
    y_next = (low_next, high_next)
    plane = Group(
        y=y_weights(even)[:2],
        y_same=y_next,
        y_next=y_next,
        **x_weights(even, odd, even_next),
    )
    link = z_link(plane, plane.moved(1), True)
    link_below = link.moved(-1)
    inner = within(plane, link_below.faces, link.faces, True)

    def around(value):
        return (pltpu.roll(value, 1, 0), value, pltpu.roll(value, 7, 0))

    own, following = z_weights(*around(even[0])), z_weights(*around(even_next[0]))
    lo, hi = (with_lanes(own[n], following[n]) for n in (0, 1))
    weights = Group(lo=lo, hi=hi, lo_same=lo[2:], hi_same=hi[2:])
    same, up, down = between(weights, inner, link_below, link)
    centre, side, inside = level(
        inner,
        (weights.moved(-1), inner.moved(-1), link_below),
        (weights.moved(1), inner.moved(1), link),
    )
    rows = (1, 3)
    merge(-1, 0, 0, same[0], rows)
    merge(-1, 0, 1, same[2], rows)
    merge(-1, 0, -1, previous_lane(same[1]), rows)
    merge(-1, -1, 0, up[0], rows)
    merge(-1, -1, 1, up[2], rows)
    merge(-1, -1, -1, previous_lane(up[1]), rows)
    rows = (3, 5)
    merge(1, 0, 0, same[0], rows)
    merge(1, 0, 1, same[1], rows)
    merge(1, 0, -1, previous_lane(same[2]), rows)
    merge(1, -1, 0, down[0], rows)
    merge(1, -1, 1, down[1], rows)
    merge(1, -1, -1, previous_lane(down[2]), rows)
    rows = (2, 4)
    merge(0, 0, 0, -centre, rows)
    merge(0, 0, 1, side, rows)
    merge(0, 0, -1, previous_lane(side), rows)
    merge(0, -1, 0, inside[0], rows)
    merge(0, -1, -1, previous_lane(inside[1]), rows)
    merge(0, -1, 1, inside[2], rows)


def split_lanes(value):
    lane = lax.broadcasted_iota(jnp.int32, (value.shape[0], 128), 1)
    left, right = value[:, :128], value[:, 128:]
    first = (lane * 2) % 128 + lane // 64
    left = jnp.take_along_axis(left, first, axis=1)
    right = jnp.take_along_axis(right, (first + 1) % 2 + first // 2 * 2, axis=1)
    even = jnp.where(lane < 64, left, right)
    odd = pltpu.roll(jnp.where(lane < 64, right, left), 64, 1)
    return even, odd


SENT = {-1: (0, 1), 0: (0, 4), 1: (2, 2)}
LANDED = {-1: 6, 0: 2, 1: 0}
AHEAD = [(-1, 1), (1, 1), (0, 1)]
SIDE = [(-1, 0), (1, 0)]
BACK = [(0, -1), (-1, -1), (1, -1)]
MESSAGES = AHEAD + SIDE + BACK


def exchange_kernel(
    material,
    diffusivity,
    variation,
    out,
    blocks,
    facts,
    levels,
    borders,
    edges,
    split,
    tiles,
    beyond,
    load_sem,
    send_sem,
    recv_sem,
    here,
):
    gz, xy = lax.axis_index("gz"), lax.axis_index("xy")
    count_z, count_x = lax.axis_size("gz"), lax.axis_size("xy")
    inputs = (material, variation)

    def exists(dz, dx):
        inside = None
        for at, step, count in ((gz, dz, count_z), (xy, dx, count_x)):
            if step:
                good = at + step < count if step > 0 else at > 0
                inside = good if inside is None else jnp.logical_and(inside, good)
        return inside

    def device(dz, dx):
        return {"gz": gz + dz, "xy": xy + dx}

    def copies(dz, dx, origin=None):
        origin = inputs if origin is None else origin
        n = MESSAGES.index((dz, dx))
        first, planes = SENT[dz]
        made = []
        for which in (0, 1):
            source = origin[which].at[pl.ds(first, planes)]
            if dx == 0:
                target = borders[which].at[pl.ds(0 if dz > 0 else 2, planes)]
            else:
                row, rows, at = (14, 2, 6) if dx > 0 else (0, 1, 0)
                source = origin[which].at[pl.ds(first, planes), pl.ds(row, rows)]
                target = edges[0 if dx > 0 else 1][which].at[pl.ds(LANDED[dz], planes), pl.ds(at, rows)]
            made.append(
                pltpu.make_async_remote_copy(
                    src_ref=source,
                    dst_ref=target,
                    send_sem=send_sem.at[n, which],
                    recv_sem=recv_sem.at[n, which],
                    device_id=device(dz, dx),
                    device_id_type=MESH,
                )
            )
        return made

    def send(dz, dx, origin=None):
        @pl.when(exists(dz, dx))
        def _():
            for copy in copies(dz, dx, origin):
                copy.start()

    def receive(dz, dx):
        @pl.when(exists(-dz, -dx))
        def _():
            for copy in copies(dz, dx):
                copy.wait_recv()

    barrier = pltpu.get_barrier_semaphore()
    place_in_row = lax.rem(xy, ROW)
    first = jnp.logical_and(place_in_row == 0, xy > 0)
    last = jnp.logical_and(place_in_row == ROW - 1, xy < count_x - 1)
    inner = jnp.logical_not(jnp.logical_or(first, last))
    not_last = jnp.logical_not(last)
    before_last = lax.rem(xy + 1, ROW) == ROW - 1
    before_last = jnp.logical_and(before_last, xy < count_x - 2)

    def greet(semaphore, dz, dx, condition=None):
        good = exists(dz, dx)

        @pl.when(good if condition is None else jnp.logical_and(good, condition))
        def _():
            pl.semaphore_signal(
                semaphore, inc=1, device_id=device(dz, dx), device_id_type=MESH
            )

    loads = [
        pltpu.make_async_copy(source, target, load_sem.at[n])
        for n, (source, target) in enumerate(
            ((material, blocks), (variation, facts), (diffusivity, levels))
        )
    ]
    one = jnp.int32(1)
    z_sides = jnp.where(gz > 0, one, 0) + jnp.where(gz < count_z - 1, one, 0)

    @pl.when(last)
    def _():
        pl.semaphore_wait(barrier, z_sides + 1)
        for dz, dx in AHEAD:
            greet(here, dz, dx)
        for dz, dx in AHEAD:
            send(dz, dx)
        for dz, dx in BACK:
            greet(barrier, dz, dx)
        for copy in loads:
            copy.start()

    @pl.when(not_last)
    def _():
        for dz, dx in BACK + SIDE:
            greet(barrier, dz, dx)
        for dz, dx in AHEAD:
            greet(barrier, dz, dx, jnp.logical_not(before_last))
        for copy in loads:
            copy.start()
        expected = (
            z_sides
            + jnp.where(xy < count_x - 1, z_sides + 1, 0)
            + jnp.where(jnp.logical_and(inner, xy > 0), z_sides + 1, 0)
        )
        pl.semaphore_wait(barrier, expected)
        for dz, dx in AHEAD + SIDE:
            send(dz, dx)

    @pl.when(inner)
    def _():
        for dz, dx in BACK:
            send(dz, dx)

    def resistivity(which, factor):
        values = table
        for bit in (1, 2, 4):
            chosen = (which & bit) != 0
            values = [
                jnp.where(chosen, values[2 * n + 1], values[2 * n])
                for n in range(len(values) // 2)
            ]
        return -0.5 / (values[0] * factor)

    def place(plane, which, factor):
        for yp, half in enumerate(split_lanes(resistivity(which, factor))):
            split[plane, yp, pl.ds(0, 16), :] = half
            for xp in (0, 1):
                rows = split[plane, yp, pl.ds(xp, 8, stride=2), :]
                tiles[xp, yp, pl.ds(8 * plane, 8), :] = rows

    for copy in loads:
        copy.wait()
    table = [levels[which] for which in range(8)]
    for k in range(4):
        place(k + 2, blocks[k], facts[k])

    @pl.when(last)
    def _():
        for dz, dx in AHEAD:
            receive(dz, dx)
        for dz, dx in BACK:
            send(dz, dx)
        for dz, dx in SIDE:
            send(dz, dx)

    for dz, dx in SIDE:
        receive(dz, dx)
    for n, plane in enumerate((0, 1, 6)):
        place(plane, borders[0][n], borders[1][n])
    for dz, dx in BACK:
        receive(dz, dx)

    @pl.when(gz == 0)
    def _():
        tiles[:, :, pl.ds(0, 16), :] = jnp.full((2, 2, 16, 128), OUTSIDE, jnp.float32)

    @pl.when(gz == count_z - 1)
    def _():
        tiles[:, :, pl.ds(48, 8), :] = jnp.full((2, 2, 8, 128), OUTSIDE, jnp.float32)

    outside = jnp.logical_or(
        jnp.logical_and(gz == 0, row_index() < 2),
        jnp.logical_and(gz == count_z - 1, row_index() == 6),
    )

    def spread(side):
        for plane in range(7):
            which, factor = (kind[plane] for kind in edges[side])
            for yp, half in enumerate(split_lanes(resistivity(which, factor))):
                beyond[side, yp, pl.ds(8 * plane, 8), :] = half

    def packed(side, row, missing):
        missing = jnp.logical_or(outside, missing)
        return [
            jnp.where(missing, OUTSIDE, beyond[side, yp, pl.ds(row, 8, stride=8), :])
            for yp in (0, 1)
        ]

    def entry(dz, dx, dy):
        return 9 * (dz + 1) + 3 * (dx + 1) + dy + 1

    def load(p, xp, yp):
        return tiles[xp, yp, pl.ds(8 * p, 8), :]

    def store(dz, dx, dy, plane, value):
        out[entry(dz, dx, dy), plane] = value

    spread(1)
    own_part(load, packed(1, 0, xy == count_x - 1), store)

    @pl.when(xy == count_x - 1)
    def _():
        for dz in (-1, 0, 1):
            for dy in (-1, 0, 1):
                for plane in (0, 1):
                    nothing = jnp.zeros((1, 128), jnp.float32)
                    out[entry(dz, 1, dy), plane, pl.ds(7, 1), :] = nothing

    @pl.when(first)
    def _():
        pl.semaphore_wait(here, z_sides + 1)
        for dz, dx in BACK:
            send(dz, dx, (blocks, facts))

    @pl.when(not_last)
    def _():
        for dz, dx in AHEAD:
            receive(dz, dx)

    spread(0)
    even_next = [tiles[0, yp, pl.ds(0, 8, stride=8), :] for yp in (0, 1)]

    def merge(dz, dx, dy, value, rows):
        if dx:
            value = jnp.where(xy > 0, value, 0.0)
        for plane, row in enumerate(rows):
            at = (entry(dz, dx, dy), plane, pl.ds(0, 1), slice(None))
            piece = value[row : row + 1, :]
            out[at] = piece if dx else out[at] + piece

    edge_part(packed(0, 6, xy == 0), packed(0, 7, xy == 0), even_next, merge)

    @pl.when(gz == 0)
    def _():
        out[0:9, 0] = jnp.zeros((9, 8, 128), jnp.float32)

    @pl.when(gz == count_z - 1)
    def _():
        out[18:27, 1] = jnp.zeros((9, 8, 128), jnp.float32)

    for dz, dx in MESSAGES:
        @pl.when(exists(dz, dx))
        def _():
            for copy in copies(dz, dx):
                copy.wait_send()


def write_kernel(result, out, sem):
    copy = pltpu.make_async_copy(result, out, sem.at[0])
    copy.start()
    copy.wait()


def per_device(material, diffusivity, variation):
    vmem = pl.BlockSpec(memory_space=pltpu.VMEM)
    material, diffusivity, variation = (
        pltpu.with_memory_space_constraint(x, pltpu.HBM)
        for x in (material, diffusivity, variation)
    )
    result = pl.pallas_call(
        exchange_kernel,
        out_shape=jax.ShapeDtypeStruct((27, 2, 8, 128), jnp.float32),
        in_specs=[
            pl.BlockSpec(memory_space=pltpu.HBM),
            pl.BlockSpec(memory_space=pltpu.HBM),
            pl.BlockSpec(memory_space=pltpu.HBM),
        ],
        out_specs=vmem,
        scratch_shapes=[
            pltpu.VMEM((4, 16, 256), jnp.int32),
            pltpu.VMEM((4, 16, 256), jnp.float32),
            pltpu.SMEM((8,), jnp.float32),
            [pltpu.VMEM((3, 16, 256), kind) for kind in (jnp.int32, jnp.float32)],
            [
                [pltpu.VMEM((7, 8, 256), kind) for kind in (jnp.int32, jnp.float32)]
                for _ in range(2)
            ],
            pltpu.VMEM((7, 2, 24, 128), jnp.float32),
            pltpu.VMEM((2, 2, 64, 128), jnp.float32),
            pltpu.VMEM((2, 2, 72, 128), jnp.float32),
            pltpu.SemaphoreType.DMA((3,)),
            pltpu.SemaphoreType.DMA((len(MESSAGES), 2)),
            pltpu.SemaphoreType.DMA((len(MESSAGES), 2)),
            pltpu.SemaphoreType.REGULAR,
        ],
        compiler_params=pltpu.CompilerParams(
            collective_id=0, has_side_effects=True, vmem_limit_bytes=VMEM_BYTES
        ),
        name="exchange",
    )(material, diffusivity, variation)
    return pl.pallas_call(
        write_kernel,
        out_shape=jax.ShapeDtypeStruct((27, 2, 8, 128), jnp.float32),
        in_specs=[vmem],
        out_specs=pl.BlockSpec(memory_space=pltpu.HBM),
        scratch_shapes=[pltpu.SemaphoreType.DMA((1,))],
        compiler_params=pltpu.CompilerParams(vmem_limit_bytes=VMEM_BYTES),
        name="write",
    )(result)


def solution(mesh):
    placed = (P("gz", "xy", None), P(), P("gz", "xy", None))
    return jax.shard_map(
        per_device, mesh=mesh, in_specs=placed, out_specs=P(None, "gz", "xy", None), check_vma=False
    )
```

```python
import functools

import jax
import jax.numpy as jnp
from jax import lax
from jax.experimental import pallas as pl
from jax.experimental.pallas import tpu as pltpu
from jax.sharding import PartitionSpec as P

MESH = pl.DeviceIdType.MESH
OUTSIDE = -1e-18
ROW = 16
VMEM_BYTES = 4 << 20


def row_index():
    return lax.broadcasted_iota(jnp.int32, (8, 128), 0)


def lane_index():
    return lax.broadcasted_iota(jnp.int32, (8, 128), 1)


def previous_row(value):
    return jnp.where(row_index() == 0, 0.0, pltpu.roll(value, 1, 0))


def next_lane(value):
    return pltpu.roll(value, 127, 1)


def previous_lane(value):
    return pltpu.roll(value, 1, 1)


def next_lane_bounded(value):
    return jnp.where(lane_index() == 127, OUTSIDE, next_lane(value))


def without_last(value):
    return jnp.where(lane_index() == 127, 0.0, value)


def inverse(value):
    return pltpu.reciprocal(value, approx=True)


class Group:
    def __init__(self, **arrays):
        self.__dict__.update(arrays)

    def moved(self, step):
        def roll(value):
            if isinstance(value, (tuple, list)):
                return tuple(roll(part) for part in value)
            return value if value is None else pltpu.roll(value, -step % 8, 0)

        return Group(**{name: roll(value) for name, value in self.__dict__.items()})


def x_weights(even, odd, even_next):
    low, high, link = [], [], []
    for yp in (0, 1):
        before = even[yp] + odd[yp]
        after = odd[yp] + even_next[yp]
        scale = inverse(before + after)
        low.append(after * scale)
        high.append(before * scale)
        link.append(scale)
    return {"low": low, "high": high, "link": link, "odd": odd, "even": even}


def y_weights(even):
    before = even[0] + even[1]
    after = even[1] + next_lane_bounded(even[0])
    scale = inverse(before + after)
    return after * scale, without_last(before * scale), before, after


def z_link(lower, upper, edge):
    steps = []
    faces = []
    for yp in (0, 1):
        odd = inverse(lower.odd[yp] + upper.odd[yp])
        low, high = lower.low[yp] * odd, lower.high[yp] * odd
        same = high * upper.high[yp]
        even = None
        if not edge:
            even = inverse(lower.even[yp] + upper.even[yp])
            same = even + low * upper.low[yp] + previous_row(same)
        steps.append((same, low * upper.high[yp], high * upper.low[yp]))
        faces.append((even, odd))
    (even_same, even_up, even_down), (odd_same, odd_up, odd_down) = steps

    def y_step(even, odd, lower_y, upper_y):
        first, second = lower_y[0] * odd, lower_y[1] * odd
        return (
            even + first * upper_y[0] + previous_lane(second * upper_y[1]),
            first * upper_y[1],
            second * upper_y[0],
        )

    return Group(
        faces=tuple(faces),
        same=y_step(even_same, odd_same, lower.y_same, upper.y_same),
        up=y_step(even_up, odd_up, lower.y, upper.y_next),
        down=y_step(even_down, odd_down, lower.y_next, upper.y),
    )


def within(plane, faces_below, faces_above, edge):
    odd_e, odd_o = plane.odd

    def lower_face(face, rho):
        return jnp.where(lane_index() == 0, inverse(rho + OUTSIDE), previous_lane(face))

    odd_before = inverse(odd_e + odd_o)
    odd_after = inverse(odd_o + next_lane_bounded(odd_e))
    odd_sum = [
        odd_before + lower_face(odd_after, odd_e) + faces_below[0][1] + faces_above[0][1],
        odd_before + odd_after + faces_below[1][1] + faces_above[1][1],
    ]
    odd_after = without_last(odd_after)
    if not edge:
        even_before, even_after = inverse(plane.before), inverse(plane.after)
        even_lower = lower_face(even_after, plane.even[0])
        even_sum = [
            even_before + even_lower + faces_below[0][0] + faces_above[0][0],
            even_before + even_after + faces_below[1][0] + faces_above[1][0],
        ]
        even_after = without_last(even_after)
    centre, along = [], []
    for yp in (0, 1):
        low, high, link = plane.low[yp], plane.high[yp], plane.link[yp]
        low_sum, high_sum = low * odd_sum[yp], high * odd_sum[yp]
        value = link + high_sum * high
        if not edge:
            value = even_sum[yp] + (link + low_sum * low) + previous_row(value)
        centre.append(value)
        along.append(link - low_sum * high)
    low_e, low_o = plane.low
    high_e, high_o = plane.high
    low_n, high_n = next_lane(low_e), next_lane(high_e)
    first, second = low_o * odd_before, high_o * odd_before
    before = (second * high_e, second * low_e, first * high_e)
    if not edge:
        before = (even_before + first * low_e + previous_row(before[0]),) + before[1:]
    first, second = low_o * odd_after, high_o * odd_after
    after = (second * high_n, first * high_n, second * low_n)
    if not edge:
        after = (even_after + first * low_n + previous_row(after[0]),) + after[1:]
    low, high = plane.y_same
    cross = low * centre[1]
    side = high * before[0] + low * after[0] - cross * high
    middle = (
        centre[0]
        + low * (cross - before[0] - before[0])
        + previous_lane(high * (high * centre[1] - after[0] - after[0]))
    )
    low, high = plane.y
    low_next, high_next = plane.y_next
    one = low * along[1] + before[1]
    two = high * along[1] + after[2]
    up = (
        along[0]
        + low_next * one
        + low * before[2]
        + previous_lane(high_next * two + high * after[1]),
        high_next * one + low * after[1],
        low_next * two + high * before[2],
    )
    return Group(centre=middle, side=side, up=up)


def z_weights(below, middle, above):
    before = below + middle
    after = middle + above
    scale = inverse(before + after)
    return after * scale, before * scale


def with_lanes(value, value_next):
    return (value, next_lane(value), value_next, next_lane(value_next))


def between(weights, inner, low_link, high_link):
    lo, lo_j, lo_i, lo_ij = weights.lo
    hi, hi_j, hi_i, hi_ij = weights.hi
    (lo_s, lo_sj), (hi_s, hi_sj) = weights.lo_same, weights.hi_same

    def term(first, second, low, high, own):
        return second * (low + first * own) + first * high

    same = (
        hi_s * (low_link.same[0] - lo_s * inner.centre) + lo_s * high_link.same[0],
        term(lo_s, hi_sj, low_link.same[1], high_link.same[1], inner.side),
        term(lo_sj, hi_s, low_link.same[2], high_link.same[2], inner.side),
    )
    up = (
        term(lo, hi_i, low_link.up[0], high_link.up[0], inner.up[0]),
        term(lo, hi_ij, low_link.up[1], high_link.up[1], inner.up[1]),
        term(lo_j, hi_i, low_link.up[2], high_link.up[2], inner.up[2]),
    )
    down = (
        term(lo_i, hi, low_link.down[0], high_link.down[0], inner.up[0]),
        term(lo_i, hi_j, low_link.down[1], high_link.down[1], inner.up[2]),
        term(lo_ij, hi, low_link.down[2], high_link.down[2], inner.up[1]),
    )
    return same, up, down


def level(own, below, above):
    centre, side = own.centre, own.side
    up = list(own.up)
    weights, inner, link = below
    hi, hi_j, hi_i, hi_ij = weights.hi
    hi_s, hi_sj = weights.hi_same
    centre = centre + hi_s * (hi_s * inner.centre - link.same[0] - link.same[0])
    side = side + hi_s * (hi_sj * inner.side + link.same[1]) + hi_sj * link.same[2]
    up[0] = up[0] + hi * (hi_i * inner.up[0] + link.up[0]) + hi_i * link.down[0]
    up[1] = up[1] + hi * (hi_ij * inner.up[1] + link.up[1]) + hi_ij * link.down[2]
    up[2] = up[2] + hi_j * (hi_i * inner.up[2] + link.up[2]) + hi_i * link.down[1]
    weights, inner, link = above
    lo, lo_j, lo_i, lo_ij = weights.lo
    lo_s, lo_sj = weights.lo_same
    centre = centre + lo_s * (lo_s * inner.centre - link.same[0] - link.same[0])
    side = side + lo_sj * (lo_s * inner.side + link.same[1]) + lo_s * link.same[2]
    up[0] = up[0] + lo_i * (lo * inner.up[0] + link.up[0]) + lo * link.down[0]
    up[1] = up[1] + lo_ij * (lo * inner.up[1] + link.up[1]) + lo * link.down[2]
    up[2] = up[2] + lo_i * (lo_j * inner.up[2] + link.up[2]) + lo_j * link.down[1]
    return centre, side, up


def own_part(load, beyond, store):
    last = row_index() == 7

    def next_row(value, packed, p):
        return jnp.where(last, packed[p : p + 1, :], pltpu.roll(value, 7, 0))

    y_beyond = y_weights(beyond)[:2]
    z_beyond = z_weights(pltpu.roll(beyond[0], 1, 0), beyond[0], pltpu.roll(beyond[0], 7, 0))
    planes = []
    for p in range(7):
        even, odd = ([load(p, xp, yp) for yp in (0, 1)] for xp in (0, 1))
        even_next = [next_row(even[yp], beyond[yp], p) for yp in (0, 1)]
        low, high, before, after = y_weights(even)
        planes.append(
            Group(
                before=before,
                after=after,
                y=(low, high),
                y_same=(low, high),
                y_next=(next_row(low, y_beyond[0], p), next_row(high, y_beyond[1], p)),
                **x_weights(even, odd, even_next),
            )
        )
    links = [z_link(planes[p], planes[p + 1], False) for p in range(6)]
    inner = [None] * 7
    for p in range(1, 6):
        inner[p] = within(planes[p], links[p - 1].faces, links[p].faces, False)
    weights = [None] * 7
    for p in (1, 3, 5):
        lo, hi = z_weights(*(planes[p + n].even[0] for n in (-1, 0, 1)))
        lo = with_lanes(lo, next_row(lo, z_beyond[0], p))
        hi = with_lanes(hi, next_row(hi, z_beyond[1], p))
        weights[p] = Group(lo=lo, hi=hi, lo_same=lo[:2], hi_same=hi[:2])
    for p in (1, 3, 5):
        same, up, down = between(weights[p], inner[p], links[p - 1], links[p])
        plane = (p - 1) // 2
        if plane < 2:
            low = functools.partial(store, -1)
            low(0, 0, plane, same[0])
            low(0, 1, plane, same[2])
            low(0, -1, plane, previous_lane(same[1]))
            low(1, 0, plane, down[0])
            low(1, 1, plane, down[2])
            low(1, -1, plane, previous_lane(down[1]))
            low(-1, 0, plane, previous_row(up[0]))
            low(-1, 1, plane, previous_row(up[2]))
            low(-1, -1, plane, previous_lane(previous_row(up[1])))
        if plane > 0:
            high = functools.partial(store, 1)
            high(0, 0, plane - 1, same[0])
            high(0, 1, plane - 1, same[1])
            high(0, -1, plane - 1, previous_lane(same[2]))
            high(1, 0, plane - 1, up[0])
            high(1, 1, plane - 1, up[1])
            high(1, -1, plane - 1, previous_lane(up[2]))
            high(-1, 0, plane - 1, previous_row(down[0]))
            high(-1, 1, plane - 1, previous_row(down[1]))
            high(-1, -1, plane - 1, previous_lane(previous_row(down[2])))
    for plane in (0, 1):
        p = 2 * plane + 2
        centre, side, up = level(
            inner[p],
            (weights[p - 1], inner[p - 1], links[p - 1]),
            (weights[p + 1], inner[p + 1], links[p]),
        )
        here = functools.partial(store, 0)
        here(0, 0, plane, -centre)
        here(0, 1, plane, side)
        here(0, -1, plane, previous_lane(side))
        here(1, 0, plane, up[0])
        here(-1, 0, plane, previous_row(up[0]))
        here(1, 1, plane, up[1])
        here(-1, -1, plane, previous_lane(previous_row(up[1])))
        here(1, -1, plane, previous_lane(up[2]))
        here(-1, 1, plane, previous_row(up[2]))


def edge_part(even, odd, even_next, merge):
    low_next, high_next = y_weights(even_next)[:2]
    y_next = (low_next, high_next)
    plane = Group(
        y=y_weights(even)[:2],
        y_same=y_next,
        y_next=y_next,
        **x_weights(even, odd, even_next),
    )
    link = z_link(plane, plane.moved(1), True)
    link_below = link.moved(-1)
    inner = within(plane, link_below.faces, link.faces, True)

    def around(value):
        return (pltpu.roll(value, 1, 0), value, pltpu.roll(value, 7, 0))

    own, following = z_weights(*around(even[0])), z_weights(*around(even_next[0]))
    lo, hi = (with_lanes(own[n], following[n]) for n in (0, 1))
    weights = Group(lo=lo, hi=hi, lo_same=lo[2:], hi_same=hi[2:])
    same, up, down = between(weights, inner, link_below, link)
    centre, side, inside = level(
        inner,
        (weights.moved(-1), inner.moved(-1), link_below),
        (weights.moved(1), inner.moved(1), link),
    )
    rows = (1, 3)
    merge(-1, 0, 0, same[0], rows)
    merge(-1, 0, 1, same[2], rows)
    merge(-1, 0, -1, previous_lane(same[1]), rows)
    merge(-1, -1, 0, up[0], rows)
    merge(-1, -1, 1, up[2], rows)
    merge(-1, -1, -1, previous_lane(up[1]), rows)
    rows = (3, 5)
    merge(1, 0, 0, same[0], rows)
    merge(1, 0, 1, same[1], rows)
    merge(1, 0, -1, previous_lane(same[2]), rows)
    merge(1, -1, 0, down[0], rows)
    merge(1, -1, 1, down[1], rows)
    merge(1, -1, -1, previous_lane(down[2]), rows)
    rows = (2, 4)
    merge(0, 0, 0, -centre, rows)
    merge(0, 0, 1, side, rows)
    merge(0, 0, -1, previous_lane(side), rows)
    merge(0, -1, 0, inside[0], rows)
    merge(0, -1, -1, previous_lane(inside[1]), rows)
    merge(0, -1, 1, inside[2], rows)


def split_lanes(value):
    lane = lax.broadcasted_iota(jnp.int32, (value.shape[0], 128), 1)
    left, right = value[:, :128], value[:, 128:]
    first = (lane * 2) % 128 + lane // 64
    left = jnp.take_along_axis(left, first, axis=1)
    right = jnp.take_along_axis(right, (first + 1) % 2 + first // 2 * 2, axis=1)
    even = jnp.where(lane < 64, left, right)
    odd = pltpu.roll(jnp.where(lane < 64, right, left), 64, 1)
    return even, odd


SENT = {-1: (0, 1), 0: (0, 4), 1: (2, 2)}
LANDED = {-1: 6, 0: 2, 1: 0}
AHEAD = [(-1, 1), (1, 1), (0, 1)]
SIDE = [(-1, 0), (1, 0)]
BACK = [(0, -1), (-1, -1), (1, -1)]
MESSAGES = AHEAD + SIDE + BACK


def exchange_kernel(
    material,
    diffusivity,
    variation,
    out,
    blocks,
    facts,
    levels,
    borders,
    low_rows,
    edges,
    split,
    tiles,
    beyond,
    load_sem,
    send_sem,
    recv_sem,
    here,
):
    gz, xy = lax.axis_index("gz"), lax.axis_index("xy")
    count_z, count_x = lax.axis_size("gz"), lax.axis_size("xy")
    inputs = (material, variation)

    def exists(dz, dx):
        inside = None
        for at, step, count in ((gz, dz, count_z), (xy, dx, count_x)):
            if step:
                good = at + step < count if step > 0 else at > 0
                inside = good if inside is None else jnp.logical_and(inside, good)
        return inside

    def device(dz, dx):
        return {"gz": gz + dz, "xy": xy + dx}

    def copies(dz, dx, origin=None):
        origin = inputs if origin is None else origin
        n = MESSAGES.index((dz, dx))
        first, planes = SENT[dz]
        made = []
        for which in (0, 1):
            source = origin[which].at[pl.ds(first, planes)]
            if dx == 0:
                target = borders[which].at[pl.ds(0 if dz > 0 else 2, planes)]
            else:
                row, rows = (14, 2) if dx > 0 else (0, 1)
                source = origin[which].at[pl.ds(first, planes), pl.ds(row, rows)]
                landing = pl.ds(LANDED[dz], planes)
                if dx > 0:
                    target = low_rows[which].at[landing]
                else:
                    target = edges[which].at[landing, pl.ds(0, 1)]
            made.append(
                pltpu.make_async_remote_copy(
                    src_ref=source,
                    dst_ref=target,
                    send_sem=send_sem.at[n, which],
                    recv_sem=recv_sem.at[n, which],
                    device_id=device(dz, dx),
                    device_id_type=MESH,
                )
            )
        return made

    def send(dz, dx, origin=None):
        @pl.when(exists(dz, dx))
        def _():
            for copy in copies(dz, dx, origin):
                copy.start()

    def receive(dz, dx):
        @pl.when(exists(-dz, -dx))
        def _():
            for copy in copies(dz, dx):
                copy.wait_recv()

    barrier = pltpu.get_barrier_semaphore()
    place_in_row = lax.rem(xy, ROW)
    first = jnp.logical_and(place_in_row == 0, xy > 0)
    last = jnp.logical_and(place_in_row == ROW - 1, xy < count_x - 1)
    inner = jnp.logical_not(jnp.logical_or(first, last))
    not_last = jnp.logical_not(last)
    before_last = lax.rem(xy + 1, ROW) == ROW - 1
    before_last = jnp.logical_and(before_last, xy < count_x - 2)

    def greet(semaphore, dz, dx, condition=None):
        good = exists(dz, dx)

        @pl.when(good if condition is None else jnp.logical_and(good, condition))
        def _():
            pl.semaphore_signal(
                semaphore, inc=1, device_id=device(dz, dx), device_id_type=MESH
            )

    loads = [
        pltpu.make_async_copy(source, target, load_sem.at[n])
        for n, (source, target) in enumerate(
            ((material, blocks), (variation, facts), (diffusivity, levels))
        )
    ]
    one = jnp.int32(1)
    z_sides = jnp.where(gz > 0, one, 0) + jnp.where(gz < count_z - 1, one, 0)

    @pl.when(last)
    def _():
        pl.semaphore_wait(barrier, z_sides + 1)
        send(*AHEAD[0])
        for dz, dx in AHEAD:
            greet(here, dz, dx)
        for dz, dx in AHEAD[1:]:
            send(dz, dx)
        for dz, dx in BACK:
            greet(barrier, dz, dx)
        for copy in loads:
            copy.start()

    @pl.when(not_last)
    def _():
        for dz, dx in BACK + SIDE:
            greet(barrier, dz, dx)
        for dz, dx in AHEAD:
            greet(barrier, dz, dx, jnp.logical_not(before_last))
        for copy in loads:
            copy.start()
        expected = (
            z_sides
            + jnp.where(xy < count_x - 1, z_sides + 1, 0)
            + jnp.where(jnp.logical_and(inner, xy > 0), z_sides + 1, 0)
        )
        pl.semaphore_wait(barrier, expected)
        for dz, dx in AHEAD + SIDE:
            send(dz, dx)

    @pl.when(inner)
    def _():
        for dz, dx in BACK:
            send(dz, dx)

    def resistivity(which, factor):
        values = table
        for bit in (1, 2, 4):
            chosen = (which & bit) != 0
            values = [
                jnp.where(chosen, values[2 * n + 1], values[2 * n])
                for n in range(len(values) // 2)
            ]
        return -0.5 * inverse(values[0] * factor)

    def place(plane, which, factor):
        for yp, half in enumerate(split_lanes(resistivity(which, factor))):
            split[plane, yp, pl.ds(0, 16), :] = half
            for xp in (0, 1):
                rows = split[plane, yp, pl.ds(xp, 8, stride=2), :]
                tiles[xp, yp, pl.ds(8 * plane, 8), :] = rows

    for copy in loads:
        copy.wait()
    table = [levels[which] for which in range(8)]
    for k in range(4):
        place(k + 2, blocks[k], facts[k])

    @pl.when(last)
    def _():
        for dz, dx in AHEAD:
            receive(dz, dx)
        for dz, dx in BACK:
            send(dz, dx)
        for dz, dx in SIDE:
            send(dz, dx)

    for dz, dx in SIDE:
        receive(dz, dx)
    for n, plane in enumerate((0, 1, 6)):
        place(plane, borders[0][n], borders[1][n])
    for dz, dx in BACK:
        receive(dz, dx)

    @pl.when(gz == 0)
    def _():
        tiles[:, :, pl.ds(0, 16), :] = jnp.full((2, 2, 16, 128), OUTSIDE, jnp.float32)

    @pl.when(gz == count_z - 1)
    def _():
        tiles[:, :, pl.ds(48, 8), :] = jnp.full((2, 2, 8, 128), OUTSIDE, jnp.float32)

    outside = jnp.logical_or(
        jnp.logical_and(gz == 0, row_index() < 2),
        jnp.logical_and(gz == count_z - 1, row_index() == 6),
    )

    def spread():
        for plane in range(7):
            which, factor = (kind[plane] for kind in edges)
            for yp, half in enumerate(split_lanes(resistivity(which, factor))):
                beyond[yp, pl.ds(8 * plane, 8), :] = half

    def bounded(halves, missing):
        missing = jnp.logical_or(outside, missing)
        return [jnp.where(missing, OUTSIDE, half) for half in halves]

    def low_row(row):
        which, factor = (kind[:, row, :] for kind in low_rows)
        return bounded(split_lanes(resistivity(which, factor)), xy == 0)

    def entry(dz, dx, dy):
        return 9 * (dz + 1) + 3 * (dx + 1) + dy + 1

    def load(p, xp, yp):
        return tiles[xp, yp, pl.ds(8 * p, 8), :]

    def store(dz, dx, dy, plane, value):
        out[entry(dz, dx, dy), plane] = value

    spread()
    high = [beyond[yp, pl.ds(0, 8, stride=8), :] for yp in (0, 1)]
    own_part(load, bounded(high, xy == count_x - 1), store)

    @pl.when(xy == count_x - 1)
    def _():
        for dz in (-1, 0, 1):
            for dy in (-1, 0, 1):
                for plane in (0, 1):
                    nothing = jnp.zeros((1, 128), jnp.float32)
                    out[entry(dz, 1, dy), plane, pl.ds(7, 1), :] = nothing

    @pl.when(first)
    def _():
        pl.semaphore_wait(here, z_sides + 1)
        for dz, dx in BACK:
            send(dz, dx, (blocks, facts))

    @pl.when(not_last)
    def _():
        for dz, dx in AHEAD:
            receive(dz, dx)

    even_next = [tiles[0, yp, pl.ds(0, 8, stride=8), :] for yp in (0, 1)]

    def merge(dz, dx, dy, value, rows):
        if dx:
            value = jnp.where(xy > 0, value, 0.0)
        for plane, row in enumerate(rows):
            at = (entry(dz, dx, dy), plane, pl.ds(0, 1), slice(None))
            piece = value[row : row + 1, :]
            out[at] = piece if dx else out[at] + piece

    edge_part(low_row(0), low_row(1), even_next, merge)

    @pl.when(gz == 0)
    def _():
        out[0:9, 0] = jnp.zeros((9, 8, 128), jnp.float32)

    @pl.when(gz == count_z - 1)
    def _():
        out[18:27, 1] = jnp.zeros((9, 8, 128), jnp.float32)

    for dz, dx in MESSAGES:
        @pl.when(exists(dz, dx))
        def _():
            for copy in copies(dz, dx):
                copy.wait_send()


def write_kernel(result, out, sem):
    copy = pltpu.make_async_copy(result, out, sem.at[0])
    copy.start()
    copy.wait()


def per_device(material, diffusivity, variation):
    vmem = pl.BlockSpec(memory_space=pltpu.VMEM)
    material, diffusivity, variation = (
        pltpu.with_memory_space_constraint(x, pltpu.HBM)
        for x in (material, diffusivity, variation)
    )
    result = pl.pallas_call(
        exchange_kernel,
        out_shape=jax.ShapeDtypeStruct((27, 2, 8, 128), jnp.float32),
        in_specs=[
            pl.BlockSpec(memory_space=pltpu.HBM),
            pl.BlockSpec(memory_space=pltpu.HBM),
            pl.BlockSpec(memory_space=pltpu.HBM),
        ],
        out_specs=vmem,
        scratch_shapes=[
            pltpu.VMEM((4, 16, 256), jnp.int32),
            pltpu.VMEM((4, 16, 256), jnp.float32),
            pltpu.SMEM((8,), jnp.float32),
            [pltpu.VMEM((3, 16, 256), kind) for kind in (jnp.int32, jnp.float32)],
            [pltpu.VMEM((8, 2, 256), kind) for kind in (jnp.int32, jnp.float32)],
            [pltpu.VMEM((7, 8, 256), kind) for kind in (jnp.int32, jnp.float32)],
            pltpu.VMEM((7, 2, 24, 128), jnp.float32),
            pltpu.VMEM((2, 2, 64, 128), jnp.float32),
            pltpu.VMEM((2, 72, 128), jnp.float32),
            pltpu.SemaphoreType.DMA((3,)),
            pltpu.SemaphoreType.DMA((len(MESSAGES), 2)),
            pltpu.SemaphoreType.DMA((len(MESSAGES), 2)),
            pltpu.SemaphoreType.REGULAR,
        ],
        compiler_params=pltpu.CompilerParams(
            collective_id=0, has_side_effects=True, vmem_limit_bytes=VMEM_BYTES
        ),
        name="exchange",
    )(material, diffusivity, variation)
    return pl.pallas_call(
        write_kernel,
        out_shape=jax.ShapeDtypeStruct((27, 2, 8, 128), jnp.float32),
        in_specs=[vmem],
        out_specs=pl.BlockSpec(memory_space=pltpu.HBM),
        scratch_shapes=[pltpu.SemaphoreType.DMA((1,))],
        compiler_params=pltpu.CompilerParams(vmem_limit_bytes=VMEM_BYTES),
        name="write",
    )(result)


def solution(mesh):
    placed = (P("gz", "xy", None), P(), P("gz", "xy", None))
    return jax.shard_map(
        per_device, mesh=mesh, in_specs=placed, out_specs=P(None, "gz", "xy", None), check_vma=False
    )
```
